128 devices in a mesh: attn: 16 (over z_hi, x, core), ffn: 8 (over z_lo, y).
Axes of the slice: x: 4, y: 4, z: 4 (z_hi: 2, z_lo: 2; z = z_hi * 2 + z_lo), core: 2. Of those that a mesh axis runs over, the one named last changes fastest.
Arguments:
- queries: bfloat16 [2, 512, 64, 256], P(None, ('attn', 'ffn')), may hold values from -128 to 128
- cache_keys: bfloat16 [2, 512, 1536, 256], P(None, ('attn', 'ffn')), may hold values from -8 to 8
- cache_values: bfloat16 [2, 512, 1536, 256], P(None, ('attn', 'ffn')), may hold values from -6 to 6
- lengths: int32 [2, 512], P(None, ('attn', 'ffn')), may hold values from 2 to 1536, as said below
- residual: bfloat16 [2, 512, 7168], P(None, None, 'ffn'), may hold values from -6 to 6
- norm_gain: bfloat16 [7168], P('ffn'), may hold values from 0.5 to 1.5
- out_weight: bfloat16 [16384, 7168], P('attn', 'ffn'), may hold values from -0.375 to 0.375
- gate_weight: bfloat16 [7168, 18432], P('ffn', 'attn'), may hold values from -0.0625 to 0.0625
- up_weight: bfloat16 [7168, 18432], P('ffn', 'attn'), may hold values from -0.0625 to 0.0625
- down_weight: bfloat16 [18432, 7168], P('attn', 'ffn'), may hold values from -0.046875 to 0.046875
Outputs:
- mixed: bfloat16 [2, 512, 7168], P(None, 'attn', 'ffn')
The draws below stay inside these ranges and needn't reach their ends.
Inputs may be any that keep to these rules, and one draw needn't show every extreme that they name: `lengths`: each micro-batch's first sequence has 1536 valid positions.
All inputs are finite; a program needn't handle non-finite values. Where the reference program divides by a largest or mean magnitude, that divisor is 1e-20 or more.
Results may differ from the reference program's by a relative error of at most 0.023.
Values may be sent and summed in bfloat16 or wider, within the bound.
No kernel may reach another device: no remote copies, remote signals or barrier semaphores. Data moves between devices by JAX's collectives and lax.ppermute only.
A program may use at most 128 MiB of HBM per device.

```python
import math
import jax
import jax.numpy as jnp
from jax import lax

D = 7168
H = 64
HD = 256
FF = 18432
QB = 128
MB = 2
R_DEV = 4
L = 1536
TOKENS = 512
N_ATTN = 16


def first_key_rows(key):
    return jax.random.normal(key, (MB, TOKENS, 1, HD), jnp.float32)


def draw_cache_keys(key, part):
    leading = first_key_rows(key)
    key = jax.random.fold_in(key, 1)
    remaining = jax.random.normal(key, (MB, TOKENS, L - 1, HD), jnp.float32)
    return jnp.clip(jnp.concatenate([leading, remaining], axis=2), -8.0, 8.0).astype(jnp.bfloat16)


def draw_queries(key, part):
    key = jax.random.fold_in(key, 2)
    normal_draw = jax.random.normal(key, (MB, TOKENS, H, HD), jnp.float32)
    return jnp.clip(normal_draw, -128.0, 128.0).astype(jnp.bfloat16)


def draw_lengths(key, part):
    key = jax.random.fold_in(key, 3)
    key_factor = jax.random.fold_in(key, 11)
    key_uniform = jax.random.fold_in(key, 12)
    factor = jax.random.randint(key_factor, (MB, TOKENS // R_DEV, 1), 1, 5)
    uniform_part = jax.random.randint(key_uniform, (MB, TOKENS // R_DEV, R_DEV), 0, L - 1)
    drawn_lengths = (2 + uniform_part * factor // 4).reshape(MB, TOKENS)
    first_column = jnp.arange(TOKENS)[None, :] == 0
    return jnp.where(first_column, L, drawn_lengths).astype(jnp.int32)


def block_scale(own_key, dims, split, low, high):
    loudness, own = 1.0, jax.random.fold_in(own_key, 6)
    for axis_at, parts in split:
        steps = jnp.exp(jax.random.uniform(jax.random.fold_in(own, axis_at), (parts,), jnp.float32, low / len(split), high / len(split)))
        loudness = loudness * jnp.repeat(steps, dims[axis_at] // parts).reshape([-1 if axis == axis_at else 1 for axis in range(len(dims))])
    return loudness


def normal_values(key, extent, scale, bound, split=(), dtype=jnp.bfloat16):
    factor_of = block_scale(key, extent, split, -0.22, 0.18) if split else 1.0
    entries = jax.random.normal(key, extent, jnp.float32) * scale * factor_of
    return jnp.minimum(jnp.maximum(entries, -bound), bound).astype(dtype)


def setup_inputs(seed: int = 0) -> dict:
    key_list = jax.random.split(jax.random.key(seed), 11)
    queries = draw_queries(jax.random.fold_in(key_list[10], 71), 0)
    cache_keys = draw_cache_keys(jax.random.fold_in(key_list[10], 71), 0)
    cache_values = normal_values(key_list[2], (MB, TOKENS, L, HD), 1.0, 6.0, ((1, 128),))
    lengths = draw_lengths(jax.random.fold_in(key_list[10], 71), 0)
    residual = normal_values(key_list[4], (MB, TOKENS, D), 1.0, 6.0, ((2, 8),))
    norm_gain = jnp.clip(1.0 + 0.1 * jax.random.normal(key_list[5], (D,), jnp.float32), 0.5, 1.5).astype(jnp.bfloat16)
    out_weight = normal_values(key_list[6], (H * HD, D), (H * HD // 64) ** -0.5, 0.375, ((0, 16), (1, 8)))
    gate_weight = normal_values(key_list[7], (D, FF), D ** -0.5, 0.0625, ((0, 8), (1, 16)))
    up_weight = normal_values(key_list[8], (D, FF), D ** -0.5, 0.0625, ((0, 8), (1, 16)))
    down_weight = normal_values(key_list[9], (FF, D), FF ** -0.5, 0.046875, ((0, 16), (1, 8)))
    return dict(queries=queries, cache_keys=cache_keys, cache_values=cache_values, lengths=lengths, residual=residual, norm_gain=norm_gain, out_weight=out_weight, gate_weight=gate_weight, up_weight=up_weight, down_weight=down_weight)


negative_fill = -1e+30

def attend_token(query_rows, key_cache, value_cache, length):
    scores = jnp.dot(query_rows, key_cache.T, preferred_element_type=jnp.float32) / math.sqrt(HD)
    valid_mask = jnp.arange(L) < length
    scores = jnp.where(valid_mask[None, :], scores, negative_fill)
    row_peak = lax.optimization_barrier(jnp.max(scores, axis=1, keepdims=True))
    weights = jnp.where(valid_mask[None, :], jnp.exp(scores - row_peak), 0.0)
    totals = lax.optimization_barrier(jnp.sum(weights, axis=1, keepdims=True))
    mixed_values = jnp.dot(weights.astype(jnp.bfloat16), value_cache, preferred_element_type=jnp.float32)
    return (mixed_values / totals).reshape(H * HD)

def decode_layer(queries, cache_keys, cache_values, lengths, residual, norm_gain, out_weight, gate_weight, up_weight, down_weight):
    attn_out = lax.map(lambda token_items: attend_token(*token_items), (queries, cache_keys, cache_values, lengths))
    blocks = attn_out.reshape(TOKENS, H * HD // QB, QB)
    block_scales = (lax.optimization_barrier(jnp.max(jnp.abs(blocks), axis=2)) + 1e-06).astype(jnp.bfloat16)
    levels = jnp.floor(127.0 * blocks / block_scales.astype(jnp.float32)[:, :, None] + 0.5)
    quantized = jnp.clip(levels, -127.0, 127.0).astype(jnp.bfloat16)
    dequantized = (quantized.astype(jnp.float32) * block_scales.astype(jnp.float32)[:, :, None] / 127.0).reshape(TOKENS, H * HD)
    group_rows = H * HD // N_ATTN
    projected = jnp.zeros((TOKENS, D), jnp.float32)
    for member in range(N_ATTN):
        selected = slice(member * group_rows, (member + 1) * group_rows)
        group_product = jnp.dot(dequantized[:, selected], out_weight[selected].astype(jnp.float32), precision=lax.Precision.HIGHEST)
        projected = projected + lax.optimization_barrier(group_product.astype(jnp.bfloat16)).astype(jnp.float32)
    stream = residual.astype(jnp.float32) + projected
    inv_rms = lax.rsqrt(lax.optimization_barrier(jnp.sum(stream * stream, axis=1)) / D + 1e-06)
    scaled = (stream * norm_gain.astype(jnp.float32)).astype(jnp.bfloat16)
    gate_sum = jnp.dot(scaled, gate_weight, preferred_element_type=jnp.float32) * inv_rms[:, None]
    up_sum = jnp.dot(scaled, up_weight, preferred_element_type=jnp.float32) * inv_rms[:, None]
    activated = (jax.nn.silu(gate_sum) * up_sum).astype(jnp.bfloat16)
    return (stream + jnp.dot(activated, down_weight, preferred_element_type=jnp.float32)).astype(jnp.bfloat16)

def reference(queries, cache_keys, cache_values, lengths, residual, norm_gain, out_weight, gate_weight, up_weight, down_weight):
    outputs = [decode_layer(queries[micro], cache_keys[micro], cache_values[micro], lengths[micro], residual[micro], norm_gain, out_weight, gate_weight, up_weight, down_weight) for micro in range(MB)]
    return jnp.stack(outputs)
```

```python
import functools
import math

import jax
import jax.numpy as jnp
from jax import lax
from jax.experimental import pallas as pl
from jax.experimental.pallas import tpu as pltpu
from jax.sharding import PartitionSpec as P

D = 7168
QB = 128
N_ATTN = 16
N_FFN = 8
NEG = -1e30
BF = jnp.bfloat16
F32 = jnp.float32
GROUPS = ((0, 1),)


def attend_kernel(len_ref, q_ref, k_ref, v_ref, o_ref):
    s = pl.program_id(0)
    q = q_ref[0]
    scores = lax.dot_general(
        q, k_ref[0], (((1,), (1,)), ((), ())), preferred_element_type=F32
    ) * (1.0 / math.sqrt(q.shape[1]))
    offsets = lax.broadcasted_iota(jnp.int32, scores.shape, 1)
    scores = jnp.where(offsets < len_ref[s], scores, NEG)
    peak = jnp.max(scores, axis=1, keepdims=True)
    weights = jnp.exp(scores - peak)
    totals = jnp.sum(weights, axis=1, keepdims=True)
    out = jnp.dot(weights.astype(BF), v_ref[0], preferred_element_type=F32) / totals
    for b in range(out.shape[1] // QB):
        block = out[:, b * QB : (b + 1) * QB]
        scale = (jnp.max(jnp.abs(block), axis=1, keepdims=True) + 1e-06).astype(BF).astype(F32)
        levels = jnp.clip(jnp.floor(127.0 * block / scale + 0.5), -127.0, 127.0)
        o_ref[0, :, b * QB : (b + 1) * QB] = (levels * scale / 127.0).astype(BF)


def attend(q, k, v, lengths):
    n, h, hd = q.shape
    l = k.shape[1]
    return pl.pallas_call(
        attend_kernel,
        out_shape=jax.ShapeDtypeStruct((n, h, hd), BF),
        grid_spec=pltpu.PrefetchScalarGridSpec(
            num_scalar_prefetch=1,
            grid=(n,),
            in_specs=[
                pl.BlockSpec((1, h, hd), lambda i, _: (i, 0, 0)),
                pl.BlockSpec((1, l, hd), lambda i, _: (i, 0, 0)),
                pl.BlockSpec((1, l, hd), lambda i, _: (i, 0, 0)),
            ],
            out_specs=pl.BlockSpec((1, h, hd), lambda i, _: (i, 0, 0)),
        ),
        compiler_params=pltpu.CompilerParams(vmem_limit_bytes=32 * 2**20),
        cost_estimate=pl.CostEstimate(
            flops=4 * n * h * l * hd, bytes_accessed=4 * n * l * hd, transcendentals=n * h * l
        ),
    )(lengths, q, k, v)


def ax(x, k):
    return lax.ppermute(x, "attn", [(i, i ^ k) for i in range(N_ATTN)])


def fx(x, k):
    return lax.ppermute(x, "ffn", [(i, i ^ k) for i in range(N_FFN)])


def total(parts):
    t = parts[0].astype(F32)
    for p in parts[1:]:
        t = t + p.astype(F32)
    return t


def flip_bits(x, axis, index):
    s = x.shape
    y = x.reshape(s[:axis] + (2, 2, 2) + s[axis + 1 :])
    for b in range(3):
        bit = (index >> (2 - b)) & 1
        y = jnp.where(bit == 1, jnp.flip(y, axis + b), y)
    return y.reshape(s)


def pick(x, i, axis):
    return lax.dynamic_index_in_dim(x, i, axis, keepdims=False)


def gather_ffn_zy(x):
    b = jnp.stack([x, fx(x, 4)])
    return jnp.stack([b] + [fx(b, k) for k in range(1, 4)], 1)


def gather_ffn_yz(x):
    b = jnp.stack([x] + [fx(x, k) for k in range(1, 4)])
    return jnp.stack([b, fx(b, 4)])


def scatter_ffn_zy(x):
    s = total([x[0], fx(x[1], 4)]).astype(BF)
    return total([s[0]] + [fx(s[k], k) for k in range(1, 4)])


def scatter_ffn_yz(x):
    s = total([x[:, 0]] + [fx(x[:, k], k) for k in range(1, 4)]).astype(BF)
    return total([s[0], fx(s[1], 4)])


def half(queries, cache_keys, cache_values, lengths, residual, gain, wo, wg, wu, wd):
    nm, r = queries.shape[:2]
    n = nm * r
    a = lax.axis_index("attn")
    f = lax.axis_index("ffn")
    zh, xi, c = a // 8, (a // 2) % 4, a % 2
    w = residual.shape[2]
    hid = wg.shape[1]

    out = attend(
        queries.reshape(n, *queries.shape[2:]),
        cache_keys.reshape(n, *cache_keys.shape[2:]),
        cache_values.reshape(n, *cache_values.shape[2:]),
        lengths.reshape(n),
    )
    groups = out.reshape(n, N_ATTN, -1).transpose(1, 0, 2)
    got = lax.all_to_all(groups, "attn", 0, 0)
    x0, x1 = got[:, :, :512], got[:, :, 512:]
    h0 = gather_ffn_zy(x0).reshape(N_FFN, N_ATTN, n, -1)
    h1 = gather_ffn_yz(x1).reshape(N_FFN, N_ATTN, n, -1)
    h0 = h0.transpose(1, 0, 2, 3).reshape(N_ATTN * N_FFN * n, -1)
    h1 = h1.transpose(1, 0, 2, 3).reshape(N_ATTN * N_FFN * n, -1)
    rows = N_FFN * n
    part = jnp.dot(h0, wo[:512], preferred_element_type=F32) + jnp.dot(
        h1, wo[512:], preferred_element_type=F32
    )
    part = part.astype(BF).reshape(8, 2, rows, w)

    other = ax(pick(part, 1 - c, 1), 1)
    s = (pick(part, c, 1).astype(F32) + other.astype(F32)).astype(BF).reshape(2, 4, rows, w)
    s = total(
        [pick(s, xi, 1)] + [ax(pick(s, xi ^ k, 1), 2 * k) for k in range(1, 4)]
    ).astype(BF)
    projected = total([pick(s, zh, 0), ax(pick(s, 1 - zh, 0), 8)])

    res = lax.dynamic_slice_in_dim(
        residual.reshape(nm, N_ATTN, N_FFN, r, w), a, 1, 1
    )[:, 0]
    res = flip_bits(res, 1, f).transpose(1, 0, 2, 3).reshape(rows, w)
    stream = res.astype(F32) + projected
    scaled = (stream * gain.astype(F32)).astype(BF)

    b = jnp.stack([scaled, ax(scaled, 8)])
    q4 = jnp.stack([b] + [ax(b, 2 * k) for k in range(1, 4)])
    full = jnp.stack([q4, ax(q4, 1)])
    full = full.reshape(N_ATTN * rows, w)
    square = jnp.sum((full.astype(F32) / gain.astype(F32)) ** 2, axis=1)
    gate = jnp.dot(full, wg, preferred_element_type=F32).astype(BF)
    up = jnp.dot(full, wu, preferred_element_type=F32).astype(BF)
    square = jnp.broadcast_to(square.astype(BF)[:, None], (N_ATTN * rows, 128))
    gate = jnp.concatenate([gate, square], axis=1)

    def by_owner(t):
        return t.reshape(N_ATTN, 2, 4, n, -1).transpose(1, 2, 0, 3, 4).reshape(
            2, 4, N_ATTN * n, -1
        )

    up_sum = scatter_ffn_zy(by_owner(up))
    gate_sum = scatter_ffn_yz(by_owner(gate))
    inv = lax.rsqrt(gate_sum[:, hid : hid + 1] / D + 1e-06)
    gate_sum = gate_sum[:, :hid]
    act = (jax.nn.silu(gate_sum * inv) * (up_sum * inv)).astype(BF)

    cut = 640
    a0 = gather_ffn_zy(act[:, :cut]).reshape(N_FFN, N_ATTN, n, -1)
    a1 = gather_ffn_yz(act[:, cut:]).reshape(N_FFN, N_ATTN, n, -1)
    a0 = a0.transpose(1, 0, 2, 3).reshape(N_ATTN * rows, -1)
    a1 = a1.transpose(1, 0, 2, 3).reshape(N_ATTN * rows, -1)
    down = jnp.dot(a0, wd[:cut], preferred_element_type=F32) + jnp.dot(
        a1, wd[cut:], preferred_element_type=F32
    )
    down = down.astype(BF).reshape(2, 4, 2, rows, w)
    s = (down[0].astype(F32) + ax(down[1], 1).astype(F32)).astype(BF)
    s = total([s[0]] + [ax(s[k], 2 * k) for k in range(1, 4)]).astype(BF)
    final = stream + total([s[0], ax(s[1], 8)])
    final = final.astype(BF).reshape(N_FFN, nm, r, w)
    final = flip_bits(final, 0, f).transpose(1, 0, 2, 3).reshape(nm, N_FFN * r, w)
    return final


def local(
    queries,
    cache_keys,
    cache_values,
    lengths,
    residual,
    norm_gain,
    out_weight,
    gate_weight,
    up_weight,
    down_weight,
):
    outs = []
    for g in GROUPS:
        sl = slice(g[0], g[-1] + 1)
        outs.append(
            half(
                queries[sl],
                cache_keys[sl],
                cache_values[sl],
                lengths[sl],
                residual[sl],
                norm_gain,
                out_weight,
                gate_weight,
                up_weight,
                down_weight,
            )
        )
    return jnp.concatenate(outs, axis=0)


def solution(mesh):
    in_specs = (
        P(None, ("attn", "ffn"), None, None),
        P(None, ("attn", "ffn"), None, None),
        P(None, ("attn", "ffn"), None, None),
        P(None, ("attn", "ffn")),
        P(None, None, "ffn"),
        P("ffn"),
        P("attn", "ffn"),
        P("ffn", "attn"),
        P("ffn", "attn"),
        P("attn", "ffn"),
    )
    out_specs = P(None, "attn", "ffn")
    return jax.shard_map(local, mesh=mesh, in_specs=in_specs, out_specs=out_specs, check_vma=False)
```

```python
import functools
import math

import jax
import jax.numpy as jnp
from jax import lax
from jax.experimental import pallas as pl
from jax.experimental.pallas import tpu as pltpu
from jax.sharding import PartitionSpec as P

D = 7168
QB = 128
N_ATTN = 16
N_FFN = 8
NQ = 8
NEG = -1e30
BF = jnp.bfloat16
F32 = jnp.float32
MIB = 2**20
PLANES = [[2 * q + c for q in range(NQ)] for c in range(2)]
ORDER = ((1, 3, 4), (3, 4, 1), (4, 1, 3))
NP = len(ORDER)


def attend_kernel(len_ref, q_ref, k_ref, v_ref, o_ref):
    s = pl.program_id(0)
    q = q_ref[0]
    scores = lax.dot_general(
        q, k_ref[0], (((1,), (1,)), ((), ())), preferred_element_type=F32
    ) * (1.0 / math.sqrt(q.shape[1]))
    offsets = lax.broadcasted_iota(jnp.int32, scores.shape, 1)
    scores = jnp.where(offsets < len_ref[s], scores, NEG)
    peak = jnp.max(scores, axis=1, keepdims=True)
    weights = jnp.exp(scores - peak)
    totals = jnp.sum(weights, axis=1, keepdims=True)
    out = jnp.dot(weights.astype(BF), v_ref[0], preferred_element_type=F32) / totals
    for b in range(out.shape[1] // QB):
        block = out[:, b * QB : (b + 1) * QB]
        scale = (jnp.max(jnp.abs(block), axis=1, keepdims=True) + 1e-06).astype(BF).astype(F32)
        levels = jnp.clip(jnp.floor(127.0 * block / scale + 0.5), -127.0, 127.0)
        o_ref[0, :, b * QB : (b + 1) * QB] = (levels * scale / 127.0).astype(BF)


def attend(q, k, v, lengths):
    n, h, hd = q.shape
    l = k.shape[1]
    return pl.pallas_call(
        attend_kernel,
        out_shape=jax.ShapeDtypeStruct((n, h, hd), BF),
        grid_spec=pltpu.PrefetchScalarGridSpec(
            num_scalar_prefetch=1,
            grid=(n,),
            in_specs=[
                pl.BlockSpec((1, h, hd), lambda i, _: (i, 0, 0)),
                pl.BlockSpec((1, l, hd), lambda i, _: (i, 0, 0)),
                pl.BlockSpec((1, l, hd), lambda i, _: (i, 0, 0)),
            ],
            out_specs=pl.BlockSpec((1, h, hd), lambda i, _: (i, 0, 0)),
        ),
        compiler_params=pltpu.CompilerParams(vmem_limit_bytes=58 * MIB),
        cost_estimate=pl.CostEstimate(
            flops=4 * n * h * l * hd, bytes_accessed=4 * n * l * hd, transcendentals=n * h * l
        ),
    )(lengths, q, k, v)


def ax(x, k):
    return lax.ppermute(x, "attn", [(i, i ^ k) for i in range(N_ATTN)])


def fx(x, k):
    return lax.ppermute(x, "ffn", [(i, i ^ k) for i in range(N_FFN)])


def over_chips(x):
    return lax.all_to_all(x, "attn", 0, 0, axis_index_groups=PLANES)


def flip_bits(x, axis, index):
    s = x.shape
    y = x.reshape(s[:axis] + (2, 2, 2) + s[axis + 1 :])
    for b in range(3):
        bit = (index >> (2 - b)) & 1
        y = jnp.where(bit == 1, jnp.flip(y, axis + b), y)
    return y.reshape(s)


def pair_rows(acc, first, second):
    return jnp.concatenate([acc[first : first + 8], acc[second : second + 8]], axis=0).astype(BF)


def column_chunks(width, step=256):
    return [(s, min(step, width - s)) for s in range(0, width, step)]


def project_kernel(core_ref, b0, r1, r2, r3, b1, t1, own_ref, sib_ref, o_ref, x_ref):
    for k, ref in enumerate((b0, r1, r2, r3)):
        for z in range(2):
            j = z * 4 + k
            x_ref[j * 32 : j * 32 + 32, :] = ref[z]
    for z, ref in enumerate((b1, t1)):
        for k in range(4):
            j = z * 4 + k
            x_ref[256 + j * 32 : 256 + j * 32 + 32, :] = ref[k]
    depth = own_ref.shape[0]
    core = core_ref[0]
    mine = x_ref[:, pl.ds(pl.multiple_of(core * depth, depth), depth)]
    other = x_ref[:, pl.ds(pl.multiple_of((1 - core) * depth, depth), depth)]
    for start, size in column_chunks(o_ref.shape[2]):
        cols = slice(start, start + size)
        acc = jnp.dot(mine, own_ref[:, cols], preferred_element_type=F32) + jnp.dot(
            other, sib_ref[:, cols], preferred_element_type=F32
        )
        for q in range(NQ):
            base = (q // 4) * 256 + (q % 4) * 8
            for t in range(4):
                o_ref[q, t * 16 : t * 16 + 16, cols] = pair_rows(
                    acc, base + 2 * t * 32, base + (2 * t + 1) * 32
                )


def vmem_specs(count):
    return [pl.BlockSpec(memory_space=pltpu.VMEM)] * count


def project(core, pieces, own, sib):
    depth, width = own.shape
    rows = NQ * 64
    return pl.pallas_call(
        project_kernel,
        out_shape=jax.ShapeDtypeStruct((NQ, 64, width), BF),
        in_specs=[pl.BlockSpec(memory_space=pltpu.SMEM)] + vmem_specs(8),
        out_specs=pl.BlockSpec(memory_space=pltpu.VMEM),
        scratch_shapes=[pltpu.VMEM((rows, 2 * depth), BF)],
        compiler_params=pltpu.CompilerParams(vmem_limit_bytes=24 * MIB),
        cost_estimate=pl.CostEstimate(
            flops=4 * rows * depth * width, bytes_accessed=6 * 2**20, transcendentals=0
        ),
    )(core.reshape(1), *pieces, own, sib)


def hidden_kernel(order, with_square, full_ref, gain_ref, g0, u0, g1, u1, send_ref, keep_ref):
    step = g0.shape[1]
    full = full_ref[...]

    def put(acc, cols):
        for b0 in range(2):
            ref = send_ref if b0 else keep_ref
            for b1 in range(2):
                for b2 in range(2):
                    j = (b0 * order[0]) ^ (b1 * order[1]) ^ (b2 * order[2])
                    for t in range(4):
                        ref[b1, b2, t * 16 : t * 16 + 16, cols] = pair_rows(
                            acc, 2 * t * 64 + j * 8, (2 * t + 1) * 64 + j * 8
                        )

    for i, w in enumerate((g0, u0, g1, u1)):
        acc = jnp.dot(full, w[...], preferred_element_type=F32)
        put(acc, slice(i * step, (i + 1) * step))
    if with_square:
        ratio = full.astype(F32) / gain_ref[...].astype(F32)
        square = jnp.sum(ratio * ratio, axis=1, keepdims=True)
        put(jnp.broadcast_to(square, (full.shape[0], 128)), slice(4 * step, 4 * step + 128))


def hidden(part, full, gain, weights):
    rows, width = full.shape
    hid = weights[0].shape[1]
    step = hid // NP
    with_square = part == NP - 1
    cols = 4 * step + (128 if with_square else 0)
    shape = jax.ShapeDtypeStruct((2, 2, rows // N_FFN, cols), BF)
    whole = pl.BlockSpec((2, 2, rows // N_FFN, cols), lambda i: (0, 0, 0, 0))
    return pl.pallas_call(
        functools.partial(hidden_kernel, ORDER[part], with_square),
        out_shape=(shape, shape),
        grid=(1,),
        in_specs=[
            pl.BlockSpec((rows, width), lambda i: (0, 0)),
            pl.BlockSpec((1, width), lambda i: (0, 0)),
        ]
        + [pl.BlockSpec((width, step), lambda i: (0, part))] * 4,
        out_specs=(whole, whole),
        compiler_params=pltpu.CompilerParams(vmem_limit_bytes=24 * MIB),
        cost_estimate=pl.CostEstimate(
            flops=2 * rows * width * cols, bytes_accessed=4 * 2**20, transcendentals=0
        ),
    )(full, gain, *weights)


def down_kernel(s0, r0, s1, r1, s2, r2, own_ref, sib_ref, o_ref, x_ref):
    hid = own_ref.shape[0]
    step = hid // NP
    for p, pair in enumerate(((s0, r0), (s1, r1), (s2, r2))):
        o = ORDER[p]
        for b0 in range(2):
            for b1 in range(2):
                for b2 in range(2):
                    j = (b0 * o[0]) ^ (b1 * o[1]) ^ (b2 * o[2])
                    rows = slice(j * 64, j * 64 + 64)
                    x_ref[rows, p * step : (p + 1) * step] = pair[b0][b1, b2, :, :step]
                    x_ref[rows, hid + p * step : hid + (p + 1) * step] = pair[b0][b1, b2, :, step:]
    mine, other = x_ref[:, :hid], x_ref[:, hid:]
    for start, size in column_chunks(o_ref.shape[2]):
        cols = slice(start, start + size)
        acc = jnp.dot(mine, own_ref[:, cols], preferred_element_type=F32) + jnp.dot(
            other, sib_ref[:, cols], preferred_element_type=F32
        )
        for q in range(NQ):
            for t in range(4):
                o_ref[q, t * 16 : t * 16 + 16, cols] = pair_rows(
                    acc, 2 * t * 64 + q * 8, (2 * t + 1) * 64 + q * 8
                )


def down(pieces, own, sib):
    hid, width = own.shape
    rows = NQ * 64
    return pl.pallas_call(
        down_kernel,
        out_shape=jax.ShapeDtypeStruct((NQ, 64, width), BF),
        in_specs=vmem_specs(8),
        out_specs=pl.BlockSpec(memory_space=pltpu.VMEM),
        scratch_shapes=[pltpu.VMEM((rows, 2 * hid), BF)],
        compiler_params=pltpu.CompilerParams(vmem_limit_bytes=24 * MIB),
        cost_estimate=pl.CostEstimate(
            flops=4 * rows * hid * width, bytes_accessed=6 * 2**20, transcendentals=0
        ),
    )(*pieces, own, sib)


def scatter_ffn(sends, keeps):
    f = lambda t: t.astype(F32)
    r1 = [fx(s, o[0]) for s, o in zip(sends, ORDER)]
    s2 = [(f(k[1]) + f(r[1])).astype(BF) for k, r in zip(keeps, r1)]
    r2 = [fx(s, o[1]) for s, o in zip(s2, ORDER)]
    s3 = [(f(k[0, 1]) + f(r[0, 1]) + f(q[1])).astype(BF) for k, r, q in zip(keeps, r1, r2)]
    r3 = [fx(s, o[2]) for s, o in zip(s3, ORDER)]
    return [
        f(k[0, 0]) + f(r[0, 0]) + f(q[0]) + f(t) for k, r, q, t in zip(keeps, r1, r2, r3)
    ]


def gather_ffn(parts):
    s = [jnp.stack([x, fx(x, o[2])]) for x, o in zip(parts, ORDER)]
    s = [jnp.stack([x, fx(x, o[1])]) for x, o in zip(s, ORDER)]
    return [t for x, o in zip(s, ORDER) for t in (x, fx(x, o[0]))]


def local(
    queries,
    cache_keys,
    cache_values,
    lengths,
    residual,
    norm_gain,
    out_weight,
    gate_weight,
    up_weight,
    down_weight,
):
    nm, r = queries.shape[:2]
    n = nm * r
    a = lax.axis_index("attn")
    f = lax.axis_index("ffn")
    core = a % 2
    w = residual.shape[2]
    rows = N_FFN * n

    out_sib = ax(out_weight, 1)
    gate_sib = ax(gate_weight, 1)
    up_sib = ax(up_weight, 1)
    down_sib = ax(down_weight, 1)

    out = attend(
        queries.reshape(n, *queries.shape[2:]),
        cache_keys.reshape(n, *cache_keys.shape[2:]),
        cache_values.reshape(n, *cache_values.shape[2:]),
        lengths.reshape(n),
    )
    got = over_chips(out.reshape(n, NQ, -1).transpose(1, 0, 2)).reshape(NQ * n, -1)

    x0, x1 = got[: rows // 2], got[rows // 2 :]
    b1 = jnp.stack([x1] + [fx(x1, k) for k in range(1, 4)])
    b0 = jnp.stack([x0, fx(x0, 4)])
    pieces = [b0] + [fx(b0, k) for k in range(1, 4)] + [b1, fx(b1, 4)]
    part = project(core, pieces, out_weight, out_sib)
    projected = jnp.sum(over_chips(part).astype(F32), axis=0)

    res = lax.dynamic_slice_in_dim(residual.reshape(nm, N_ATTN, N_FFN, r, w), a, 1, 1)[:, 0]
    res = flip_bits(res, 1, f).transpose(1, 0, 2, 3).reshape(rows, w)
    stream = res.astype(F32) + projected
    scaled = (stream * norm_gain.astype(F32)).astype(BF)
    full = over_chips(jnp.broadcast_to(scaled[None], (NQ, rows, w))).reshape(NQ * rows, w)

    weights = (gate_weight, up_weight, gate_sib, up_sib)
    gain = norm_gain.reshape(1, w)
    sends, keeps = zip(*[hidden(p, full, gain, weights) for p in range(NP)])
    sums = scatter_ffn(sends, keeps)
    step = gate_weight.shape[1] // NP
    inv = lax.rsqrt(sums[-1][:, 4 * step : 4 * step + 1] / D + 1e-06)
    acts = []
    for t in sums:
        g0, u0, g1, u1 = [t[:, i * step : (i + 1) * step] * inv for i in range(4)]
        acts.append(
            jnp.concatenate([jax.nn.silu(g0) * u0, jax.nn.silu(g1) * u1], axis=1).astype(BF)
        )
    part = down(gather_ffn(acts), down_weight, down_sib)
    final = stream + jnp.sum(over_chips(part).astype(F32), axis=0)
    final = final.astype(BF).reshape(N_FFN, nm, r, w)
    return flip_bits(final, 0, f).transpose(1, 0, 2, 3).reshape(nm, N_FFN * r, w)


def solution(mesh):
    in_specs = (
        P(None, ("attn", "ffn"), None, None),
        P(None, ("attn", "ffn"), None, None),
        P(None, ("attn", "ffn"), None, None),
        P(None, ("attn", "ffn")),
        P(None, None, "ffn"),
        P("ffn"),
        P("attn", "ffn"),
        P("ffn", "attn"),
        P("ffn", "attn"),
        P("attn", "ffn"),
    )
    out_specs = P(None, "attn", "ffn")
    return jax.shard_map(local, mesh=mesh, in_specs=in_specs, out_specs=out_specs, check_vma=False)
```

```python
import functools
import math

import jax
import jax.numpy as jnp
from jax import lax
from jax.experimental import pallas as pl
from jax.experimental.pallas import tpu as pltpu
from jax.sharding import PartitionSpec as P

D = 7168
QB = 128
N_ATTN = 16
N_FFN = 8
NQ = 8
NEG = -1e30
BF = jnp.bfloat16
F32 = jnp.float32
MIB = 2**20
PLANES = [[2 * q + c for q in range(NQ)] for c in range(2)]
ORDER = ((1, 3, 4), (3, 4, 1), (4, 1, 3))
NP = len(ORDER)


def attend_kernel(len_ref, q_ref, k_hbm, v_hbm, o_ref, k_ref, v_ref, k_sem, v_sem):
    nm, r, h, hd = q_ref.shape
    l = k_ref.shape[1]
    for i in range(nm * r):
        m, t = divmod(i, r)
        pltpu.make_async_copy(k_hbm.at[m, t], k_ref.at[i], k_sem.at[i]).start()
        pltpu.make_async_copy(v_hbm.at[m, t], v_ref.at[i], v_sem.at[i]).start()
    offsets = lax.broadcasted_iota(jnp.int32, (h, l), 1)

    @pl.loop(0, nm * r // 2)
    def _(step):
        outs = []
        for u in range(2):
            i = step * 2 + u
            m, t = i // r, i % r
            pltpu.make_async_copy(k_hbm.at[m, t], k_ref.at[i], k_sem.at[i]).wait()
            pltpu.make_async_copy(v_hbm.at[m, t], v_ref.at[i], v_sem.at[i]).wait()
        for u in range(2):
            i = step * 2 + u
            m, t = i // r, i % r
            scores = lax.dot_general(
                q_ref[m, t], k_ref[i], (((1,), (1,)), ((), ())), preferred_element_type=F32
            ) * (1.0 / math.sqrt(hd))
            scores = jnp.where(offsets < len_ref[m, t], scores, NEG)
            weights = jnp.exp(scores - jnp.max(scores, axis=1, keepdims=True))
            totals = jnp.sum(weights, axis=1, keepdims=True)
            outs.append(
                jnp.dot(weights.astype(BF), v_ref[i], preferred_element_type=F32) / totals
            )
        for u in range(2):
            for b in range(hd // QB):
                cols = slice(b * QB, (b + 1) * QB)
                block = outs[u][:, cols]
                peak = jnp.max(jnp.abs(block), axis=1, keepdims=True)
                scale = (peak + 1e-06).astype(BF).astype(F32)
                levels = jnp.clip(jnp.floor(127.0 * block / scale + 0.5), -127.0, 127.0)
                o_ref[step * 2 + u, :, cols] = (levels * scale / 127.0).astype(BF)


def attend(q, k, v, lengths):
    nm, r, h, hd = q.shape
    n, l = nm * r, k.shape[2]
    return pl.pallas_call(
        attend_kernel,
        out_shape=jax.ShapeDtypeStruct((n, h, hd), BF),
        in_specs=[
            pl.BlockSpec(memory_space=pltpu.SMEM),
            pl.BlockSpec(memory_space=pltpu.VMEM),
            pl.BlockSpec(memory_space=pl.ANY),
            pl.BlockSpec(memory_space=pl.ANY),
        ],
        out_specs=pl.BlockSpec(memory_space=pltpu.VMEM),
        scratch_shapes=[
            pltpu.VMEM((n, l, hd), BF),
            pltpu.VMEM((n, l, hd), BF),
            pltpu.SemaphoreType.DMA((n,)),
            pltpu.SemaphoreType.DMA((n,)),
        ],
        compiler_params=pltpu.CompilerParams(vmem_limit_bytes=58 * MIB),
        cost_estimate=pl.CostEstimate(
            flops=4 * n * h * l * hd, bytes_accessed=4 * n * l * hd, transcendentals=n * h * l
        ),
    )(lengths, q, k, v)


def ax(x, k):
    return lax.ppermute(x, "attn", [(i, i ^ k) for i in range(N_ATTN)])


def fx(x, k):
    return lax.ppermute(x, "ffn", [(i, i ^ k) for i in range(N_FFN)])


def over_chips(x):
    return lax.all_to_all(x, "attn", 0, 0, axis_index_groups=PLANES)


def vmem_specs(count):
    return [pl.BlockSpec(memory_space=pltpu.VMEM)] * count


def any_specs(count):
    return [pl.BlockSpec(memory_space=pl.ANY)] * count


SMEM = pl.BlockSpec(memory_space=pltpu.SMEM)


def column_chunks(width, step=256):
    return [(s, min(step, width - s)) for s in range(0, width, step)]


def rows_at(start, size):
    return pl.ds(pl.multiple_of(start, size), size)


def spread(at_ref, x_ref, groups, put):
    f = at_ref[1]
    per = x_ref.shape[0] // N_FFN
    for p, (near, far) in enumerate(zip(groups[0::2], groups[1::2])):
        o = ORDER[p]
        for b0, ref in enumerate((near, far)):
            for b1 in range(2):
                for b2 in range(2):
                    j = (b0 * o[0]) ^ (b1 * o[1]) ^ (b2 * o[2])
                    put(rows_at((f ^ j) * per, per), p, ref[b1, b2])


def project_kernel(at_ref, s0, r0, s1, r1, s2, r2, own_hbm, sib_hbm, o_ref, x_ref, w_ref, sem):
    copies = [
        pltpu.make_async_copy(src, w_ref.at[i], sem.at[i])
        for i, src in enumerate((own_hbm, sib_hbm))
    ]
    for copy in copies:
        copy.start()

    def put(rows, p, piece):
        x_ref[rows, PROJECT_CUTS[p] : PROJECT_CUTS[p + 1]] = piece

    spread(at_ref, x_ref, (s0, r0, s1, r1, s2, r2), put)
    for copy in copies:
        copy.wait()
    core = at_ref[0]
    depth = w_ref.shape[1]
    mine = x_ref[:, rows_at(core * depth, depth)]
    other = x_ref[:, rows_at((1 - core) * depth, depth)]
    for start, size in column_chunks(o_ref.shape[2]):
        cols = slice(start, start + size)
        acc = jnp.dot(mine, w_ref[0, :, cols], preferred_element_type=F32) + jnp.dot(
            other, w_ref[1, :, cols], preferred_element_type=F32
        )
        for q in range(NQ):
            for t in range(4):
                first = 2 * t * 64 + q * 8
                o_ref[q, t * 16 : t * 16 + 16, cols] = jnp.concatenate(
                    [acc[first : first + 8], acc[first + 64 : first + 72]], axis=0
                ).astype(BF)


def project(at, pieces, own, sib):
    depth, width = own.shape
    rows = NQ * 64
    return pl.pallas_call(
        project_kernel,
        out_shape=jax.ShapeDtypeStruct((NQ, 64, width), BF),
        in_specs=[SMEM] + vmem_specs(6) + any_specs(2),
        out_specs=pl.BlockSpec(memory_space=pltpu.VMEM),
        scratch_shapes=[
            pltpu.VMEM((rows, 2 * depth), BF),
            pltpu.VMEM((2, depth, width), BF),
            pltpu.SemaphoreType.DMA((2,)),
        ],
        compiler_params=pltpu.CompilerParams(vmem_limit_bytes=LIMIT),
        cost_estimate=pl.CostEstimate(
            flops=4 * rows * depth * width, bytes_accessed=6 * MIB, transcendentals=0
        ),
    )(at, *pieces, own, sib)


def stream_kernel(got_ref, res_ref, gain_ref, stream_ref, scaled_ref):
    total = res_ref[...].astype(F32)
    for i in range(NQ):
        total = total + got_ref[i].astype(F32)
    stream_ref[...] = total
    scaled_ref[...] = (total * gain_ref[...].astype(F32)).astype(BF)


def residual_stream(got, res, gain):
    _, rows, width = got.shape
    return pl.pallas_call(
        stream_kernel,
        out_shape=(
            jax.ShapeDtypeStruct((rows, width), F32),
            jax.ShapeDtypeStruct((rows, width), BF),
        ),
        in_specs=vmem_specs(3),
        out_specs=tuple(vmem_specs(2)),
        compiler_params=pltpu.CompilerParams(vmem_limit_bytes=16 * MIB),
    )(got, res, gain)


def hidden_kernel(at_ref, p0, p1, p2, p3, gain_ref, g0, u0, g1, u1, *refs):
    outs, (x_ref, w_ref, sem) = refs[:-3], refs[-3:]
    step = w_ref.shape[2]
    weights, copies = (g0, u0, g1, u1), []
    for part in range(NP):
        for w, third in HIDDEN_BLOCKS[part]:
            i = len(copies)
            src = weights[w].at[:, pl.ds(third * step, step)]
            copies.append(pltpu.make_async_copy(src, w_ref.at[i], sem.at[i]))
            copies[-1].start()
    f, q = at_ref[1], at_ref[2]
    for k, ref in enumerate((p0, p1, p2, p3)):
        for z in range(2):
            x_ref[rows_at((f ^ q ^ (z * 4 + k)) * 64, 64), :] = ref[z]
    full = x_ref[...]

    def put(acc, part, cols):
        o = ORDER[part]
        for b0 in range(2):
            ref = outs[2 * part + 1 - b0]
            for b1 in range(2):
                for b2 in range(2):
                    j = (b0 * o[0]) ^ (b1 * o[1]) ^ (b2 * o[2])
                    ref[b1, b2, :, cols] = acc[j * 64 : j * 64 + 64].astype(BF)

    ratio = full.astype(F32) / gain_ref[...].astype(F32)
    square = jnp.sum(ratio * ratio, axis=1, keepdims=True)
    put(jnp.broadcast_to(square, (full.shape[0], 128)), SQUARE_PART, slice(4 * step, 4 * step + 128))
    for i, copy in enumerate(copies):
        copy.wait()
        acc = jnp.dot(full, w_ref[i], preferred_element_type=F32)
        put(acc, i // 4, slice((i % 4) * step, (i % 4 + 1) * step))


HIDDEN_BLOCKS = (
    ((0, 0), (1, 0), (0, 1), (1, 1)),
    ((0, 2), (1, 2), (2, 0), (3, 0)),
    ((2, 1), (3, 1), (2, 2), (3, 2)),
)
SQUARE_PART = 2
PROJECT_CUTS = (0, 768, 1408, 2048)
LIMIT = 48 * MIB


def hidden(at, pieces, gain, weights):
    width, hid = weights[0].shape
    step, rows = hid // NP, NQ * 64
    shapes = []
    for part in range(NP):
        cols = 4 * step + (128 if part == SQUARE_PART else 0)
        shapes += [jax.ShapeDtypeStruct((2, 2, 64, cols), BF)] * 2
    outs = pl.pallas_call(
        hidden_kernel,
        out_shape=tuple(shapes),
        in_specs=[SMEM] + vmem_specs(5) + any_specs(4),
        out_specs=tuple(vmem_specs(2 * NP)),
        scratch_shapes=[
            pltpu.VMEM((rows, width), BF),
            pltpu.VMEM((4 * NP, width, step), BF),
            pltpu.SemaphoreType.DMA((4 * NP,)),
        ],
        compiler_params=pltpu.CompilerParams(vmem_limit_bytes=LIMIT),
        cost_estimate=pl.CostEstimate(
            flops=8 * rows * width * hid, bytes_accessed=14 * MIB, transcendentals=0
        ),
    )(at, *pieces, gain, *weights)
    return outs[0::2], outs[1::2]


def down_kernel(at_ref, s0, r0, s1, r1, s2, r2, own_hbm, sib_hbm, o_ref, x_ref, w_ref, sem):
    copies = [
        pltpu.make_async_copy(src, w_ref.at[i], sem.at[i])
        for i, src in enumerate((own_hbm, sib_hbm))
    ]
    for copy in copies:
        copy.start()
    step = s0.shape[3]

    def put(rows, p, piece):
        x_ref[rows, p * step : (p + 1) * step] = piece

    spread(at_ref, x_ref, (s0, r0, s1, r1, s2, r2), put)
    for copy in copies:
        copy.wait()
    hid = w_ref.shape[1]
    mine, other = x_ref[:, :hid], x_ref[:, hid:]
    for start, size in column_chunks(o_ref.shape[1]):
        cols = slice(start, start + size)
        acc = jnp.dot(mine, w_ref[0, :, cols], preferred_element_type=F32) + jnp.dot(
            other, w_ref[1, :, cols], preferred_element_type=F32
        )
        o_ref[:, cols] = acc.astype(BF)


def down(at, pieces, own, sib):
    hid, width = own.shape
    rows = NQ * 64
    return pl.pallas_call(
        down_kernel,
        out_shape=jax.ShapeDtypeStruct((rows, width), BF),
        in_specs=[SMEM] + vmem_specs(6) + any_specs(2),
        out_specs=pl.BlockSpec(memory_space=pltpu.VMEM),
        scratch_shapes=[
            pltpu.VMEM((rows, 2 * hid), BF),
            pltpu.VMEM((2, hid, width), BF),
            pltpu.SemaphoreType.DMA((2,)),
        ],
        compiler_params=pltpu.CompilerParams(vmem_limit_bytes=LIMIT),
        cost_estimate=pl.CostEstimate(
            flops=4 * rows * hid * width, bytes_accessed=6 * MIB, transcendentals=0
        ),
    )(at, *pieces, own, sib)


def scatter_ffn(sends, keeps):
    f = lambda t: t.astype(F32)
    r1 = [fx(s, o[0]) for s, o in zip(sends, ORDER)]
    s2 = [(f(k[1]) + f(r[1])).astype(BF) for k, r in zip(keeps, r1)]
    r2 = [fx(s, o[1]) for s, o in zip(s2, ORDER)]
    s3 = [(f(k[0, 1]) + f(r[0, 1]) + f(q[1])).astype(BF) for k, r, q in zip(keeps, r1, r2)]
    r3 = [fx(s, o[2]) for s, o in zip(s3, ORDER)]
    return [
        f(k[0, 0]) + f(r[0, 0]) + f(q[0]) + f(t) for k, r, q, t in zip(keeps, r1, r2, r3)
    ]


def gather_ffn(parts):
    s = [jnp.stack([x, fx(x, o[2])]) for x, o in zip(parts, ORDER)]
    s = [jnp.stack([x, fx(x, o[1])]) for x, o in zip(s, ORDER)]
    return [t for x, o in zip(s, ORDER) for t in (x, fx(x, o[0]))]


def local(
    queries,
    cache_keys,
    cache_values,
    lengths,
    residual,
    norm_gain,
    out_weight,
    gate_weight,
    up_weight,
    down_weight,
):
    nm, r = queries.shape[:2]
    n = nm * r
    a = lax.axis_index("attn")
    f = lax.axis_index("ffn")
    at = jnp.stack([a % 2, f, a // 2]).astype(jnp.int32)
    w = residual.shape[2]
    rows = N_FFN * n

    out_sib = ax(out_weight, 1)
    gate_sib = ax(gate_weight, 1)
    up_sib = ax(up_weight, 1)
    down_sib = ax(down_weight, 1)

    res = lax.dynamic_slice_in_dim(residual, a * (N_FFN * r), N_FFN * r, 1)
    res = res.reshape(nm, N_FFN, r, w).transpose(1, 0, 2, 3).reshape(rows, w)
    gain = norm_gain.reshape(1, w)

    out = attend(queries, cache_keys, cache_values, lengths)
    got = over_chips(out.reshape(n, NQ, -1).transpose(1, 0, 2)).reshape(NQ * n, -1)

    got, out_sib, gate_sib, up_sib, down_sib = lax.optimization_barrier(
        (got, out_sib, gate_sib, up_sib, down_sib)
    )
    pieces = gather_ffn([got[:, x:y] for x, y in zip(PROJECT_CUTS, PROJECT_CUTS[1:])])
    part = project(at, pieces, out_weight, out_sib)
    stream, scaled = residual_stream(over_chips(part), res, gain)

    pair = jnp.stack([scaled, ax(scaled, 8)])
    pieces = [pair] + [ax(pair, 2 * k) for k in range(1, 4)]
    weights = (gate_weight, up_weight, gate_sib, up_sib)
    sends, keeps = hidden(at, pieces, gain, weights)
    sums = scatter_ffn(sends, keeps)
    step = gate_weight.shape[1] // NP
    inv = lax.rsqrt(sums[SQUARE_PART][:, 4 * step : 4 * step + 1] / D + 1e-06)
    acts = []
    for t in sums:
        g0, u0, g1, u1 = [t[:, i * step : (i + 1) * step] * inv for i in range(4)]
        acts.append(
            jnp.concatenate([jax.nn.silu(g0) * u0, jax.nn.silu(g1) * u1], axis=1).astype(BF)
        )
    part = down(at, gather_ffn(acts), down_weight, down_sib).reshape(NQ, rows, w)
    final = stream + jnp.sum(over_chips(part).astype(F32), axis=0)
    final = final.astype(BF).reshape(N_FFN, nm, r, w)
    return final.transpose(1, 0, 2, 3).reshape(nm, N_FFN * r, w)


def solution(mesh):
    in_specs = (
        P(None, ("attn", "ffn"), None, None),
        P(None, ("attn", "ffn"), None, None),
        P(None, ("attn", "ffn"), None, None),
        P(None, ("attn", "ffn")),
        P(None, None, "ffn"),
        P("ffn"),
        P("attn", "ffn"),
        P("ffn", "attn"),
        P("ffn", "attn"),
        P("attn", "ffn"),
    )
    out_specs = P(None, "attn", "ffn")
    return jax.shard_map(local, mesh=mesh, in_specs=in_specs, out_specs=out_specs, check_vma=False)
```

```python
import functools
import math

import jax
import jax.numpy as jnp
from jax import lax
from jax.experimental import pallas as pl
from jax.experimental.pallas import tpu as pltpu
from jax.sharding import PartitionSpec as P

D = 7168
QB = 128
N_ATTN = 16
N_FFN = 8
NQ = 8
NEG = -1e30
BF = jnp.bfloat16
F32 = jnp.float32
MIB = 2**20
PLANES = [[2 * q + c for q in range(NQ)] for c in range(2)]
ORDER = ((1, 3, 4), (3, 4, 1), (4, 1, 3))
NP = len(ORDER)


def attend_kernel(len_ref, q_ref, k_hbm, v_hbm, o_ref, k_ref, v_ref, k_sem, v_sem):
    nm, r, h, hd = q_ref.shape
    l = k_ref.shape[1]
    for i in range(nm * r):
        m, t = divmod(i, r)
        pltpu.make_async_copy(k_hbm.at[m, t], k_ref.at[i], k_sem.at[i]).start()
        pltpu.make_async_copy(v_hbm.at[m, t], v_ref.at[i], v_sem.at[i]).start()
    offsets = lax.broadcasted_iota(jnp.int32, (h, l), 1)

    @pl.loop(0, nm * r // 2)
    def _(step):
        outs = []
        for u in range(2):
            i = step * 2 + u
            m, t = i // r, i % r
            pltpu.make_async_copy(k_hbm.at[m, t], k_ref.at[i], k_sem.at[i]).wait()
            pltpu.make_async_copy(v_hbm.at[m, t], v_ref.at[i], v_sem.at[i]).wait()
        for u in range(2):
            i = step * 2 + u
            m, t = i // r, i % r
            scores = lax.dot_general(
                q_ref[m, t], k_ref[i], (((1,), (1,)), ((), ())), preferred_element_type=F32
            ) * (1.0 / math.sqrt(hd))
            scores = jnp.where(offsets < len_ref[m, t], scores, NEG)
            weights = jnp.exp(scores - jnp.max(scores, axis=1, keepdims=True))
            totals = jnp.sum(weights, axis=1, keepdims=True)
            outs.append(
                jnp.dot(weights.astype(BF), v_ref[i], preferred_element_type=F32) / totals
            )
        for u in range(2):
            for b in range(hd // QB):
                cols = slice(b * QB, (b + 1) * QB)
                block = outs[u][:, cols]
                peak = jnp.max(jnp.abs(block), axis=1, keepdims=True)
                scale = (peak + 1e-06).astype(BF).astype(F32)
                levels = jnp.clip(jnp.floor(127.0 * block / scale + 0.5), -127.0, 127.0)
                o_ref[step * 2 + u, :, cols] = (levels * scale / 127.0).astype(BF)


def attend(q, k, v, lengths):
    nm, r, h, hd = q.shape
    n, l = nm * r, k.shape[2]
    return pl.pallas_call(
        attend_kernel,
        out_shape=jax.ShapeDtypeStruct((n, h, hd), BF),
        in_specs=[
            pl.BlockSpec(memory_space=pltpu.SMEM),
            pl.BlockSpec(memory_space=pltpu.VMEM),
            pl.BlockSpec(memory_space=pltpu.HBM),
            pl.BlockSpec(memory_space=pltpu.HBM),
        ],
        out_specs=pl.BlockSpec(memory_space=pltpu.VMEM),
        scratch_shapes=[
            pltpu.VMEM((n, l, hd), BF),
            pltpu.VMEM((n, l, hd), BF),
            pltpu.SemaphoreType.DMA((n,)),
            pltpu.SemaphoreType.DMA((n,)),
        ],
        compiler_params=pltpu.CompilerParams(vmem_limit_bytes=58 * MIB),
        cost_estimate=pl.CostEstimate(
            flops=4 * n * h * l * hd, bytes_accessed=4 * n * l * hd, transcendentals=n * h * l
        ),
    )(lengths, q, k, v)


def ax(x, k):
    return lax.ppermute(x, "attn", [(i, i ^ k) for i in range(N_ATTN)])


def fx(x, k):
    return lax.ppermute(x, "ffn", [(i, i ^ k) for i in range(N_FFN)])


def over_chips(x):
    return lax.all_to_all(x, "attn", 0, 0, axis_index_groups=PLANES)


def vmem_specs(count):
    return [pl.BlockSpec(memory_space=pltpu.VMEM)] * count


SMEM = pl.BlockSpec(memory_space=pltpu.SMEM)


def column_chunks(width, step=256):
    return [(s, min(step, width - s)) for s in range(0, width, step)]


def rows_at(start, size):
    return pl.ds(pl.multiple_of(start, size), size)


def spread(at_ref, x_ref, groups, put):
    f = at_ref[1]
    per = x_ref.shape[0] // N_FFN
    for p, (near, far) in enumerate(zip(groups[0::2], groups[1::2])):
        o = ORDER[p]
        for b0, ref in enumerate((near, far)):
            for b1 in range(2):
                for b2 in range(2):
                    j = (b0 * o[0]) ^ (b1 * o[1]) ^ (b2 * o[2])
                    put(rows_at((f ^ j) * per, per), p, ref[b1, b2])


def project_kernel(at_ref, s0, r0, s1, r1, s2, r2, low_ref, high_ref, o_ref, x_ref):
    def put(rows, p, piece):
        x_ref[rows, PROJECT_CUTS[p] : PROJECT_CUTS[p + 1]] = piece

    spread(at_ref, x_ref, (s0, r0, s1, r1, s2, r2), put)
    depth = low_ref.shape[0]
    low, high = x_ref[:, :depth], x_ref[:, depth:]
    for start, size in column_chunks(o_ref.shape[2]):
        cols = slice(start, start + size)
        acc = jnp.dot(low, low_ref[:, cols], preferred_element_type=F32) + jnp.dot(
            high, high_ref[:, cols], preferred_element_type=F32
        )
        for q in range(NQ):
            for t in range(4):
                first = 2 * t * 64 + q * 8
                o_ref[q, t * 16 : t * 16 + 16, cols] = jnp.concatenate(
                    [acc[first : first + 8], acc[first + 64 : first + 72]], axis=0
                ).astype(BF)


def project(at, pieces, low, high):
    depth, width = low.shape
    rows = NQ * 64
    return pl.pallas_call(
        project_kernel,
        out_shape=jax.ShapeDtypeStruct((NQ, 64, width), BF),
        in_specs=[SMEM] + vmem_specs(8),
        out_specs=pl.BlockSpec(memory_space=pltpu.VMEM),
        scratch_shapes=[pltpu.VMEM((rows, 2 * depth), BF)],
        compiler_params=pltpu.CompilerParams(vmem_limit_bytes=24 * MIB),
        cost_estimate=pl.CostEstimate(
            flops=4 * rows * depth * width, bytes_accessed=6 * MIB, transcendentals=0
        ),
    )(at, *pieces, low, high)


def stream_kernel(got_ref, res_ref, gain_ref, stream_ref, scaled_ref):
    total = res_ref[...].astype(F32)
    for i in range(NQ):
        total = total + got_ref[i].astype(F32)
    stream_ref[...] = total
    scaled_ref[...] = (total * gain_ref[...].astype(F32)).astype(BF)


def residual_stream(got, res, gain):
    _, rows, width = got.shape
    return pl.pallas_call(
        stream_kernel,
        out_shape=(
            jax.ShapeDtypeStruct((rows, width), F32),
            jax.ShapeDtypeStruct((rows, width), BF),
        ),
        in_specs=vmem_specs(3),
        out_specs=tuple(vmem_specs(2)),
        compiler_params=pltpu.CompilerParams(vmem_limit_bytes=16 * MIB),
    )(got, res, gain)


def hidden_kernel(at_ref, p0, p1, p2, p3, gain_ref, g0, u0, g1, u1, *refs):
    outs, x_ref = refs[:-1], refs[-1]
    step = g0.shape[1] // NP
    f, q = at_ref[1], at_ref[2]
    for k, ref in enumerate((p0, p1, p2, p3)):
        for z in range(2):
            x_ref[rows_at((f ^ q ^ (z * 4 + k)) * 64, 64), :] = ref[z]
    full = x_ref[...]

    def put(acc, part, start):
        o = ORDER[part]
        cols = slice(start, start + acc.shape[1])
        for b0 in range(2):
            ref = outs[2 * part + 1 - b0]
            for b1 in range(2):
                for b2 in range(2):
                    j = (b0 * o[0]) ^ (b1 * o[1]) ^ (b2 * o[2])
                    ref[b1, b2, :, cols] = acc[j * 64 : j * 64 + 64].astype(BF)

    ratio = full.astype(F32) / gain_ref[...].astype(F32)
    square = jnp.sum(ratio * ratio, axis=1, keepdims=True)
    put(jnp.broadcast_to(square, (full.shape[0], 128)), SQUARE_PART, 4 * step)
    for i, w in enumerate((g0, u0, g1, u1)):
        acc = jnp.dot(full, w[...], preferred_element_type=F32)
        for part in range(NP):
            put(acc[:, part * step : (part + 1) * step], part, i * step)


SQUARE_PART = 2
PROJECT_CUTS = (0, 768, 1408, 2048)


def hidden(at, pieces, gain, weights):
    width, hid = weights[0].shape
    step, rows = hid // NP, NQ * 64
    shapes = []
    for part in range(NP):
        cols = 4 * step + (128 if part == SQUARE_PART else 0)
        shapes += [jax.ShapeDtypeStruct((2, 2, 64, cols), BF)] * 2
    outs = pl.pallas_call(
        hidden_kernel,
        out_shape=tuple(shapes),
        in_specs=[SMEM] + vmem_specs(9),
        out_specs=tuple(vmem_specs(2 * NP)),
        scratch_shapes=[pltpu.VMEM((rows, width), BF)],
        compiler_params=pltpu.CompilerParams(vmem_limit_bytes=24 * MIB),
        cost_estimate=pl.CostEstimate(
            flops=8 * rows * width * hid, bytes_accessed=14 * MIB, transcendentals=0
        ),
    )(at, *pieces, gain, *weights)
    return outs[0::2], outs[1::2]


def down_kernel(at_ref, s0, r0, s1, r1, s2, r2, low_ref, high_ref, o_ref, x_ref):
    hid = low_ref.shape[0]
    step = hid // NP

    def put(rows, p, piece):
        x_ref[rows, p * step : (p + 1) * step] = piece[:, :step]
        x_ref[rows, hid + p * step : hid + (p + 1) * step] = piece[:, step:]

    spread(at_ref, x_ref, (s0, r0, s1, r1, s2, r2), put)
    low, high = x_ref[:, :hid], x_ref[:, hid:]
    for start, size in column_chunks(o_ref.shape[1]):
        cols = slice(start, start + size)
        acc = jnp.dot(low, low_ref[:, cols], preferred_element_type=F32) + jnp.dot(
            high, high_ref[:, cols], preferred_element_type=F32
        )
        o_ref[:, cols] = acc.astype(BF)


def down(at, pieces, low, high):
    hid, width = low.shape
    rows = NQ * pieces[0].shape[2]
    return pl.pallas_call(
        down_kernel,
        out_shape=jax.ShapeDtypeStruct((rows, width), BF),
        in_specs=[SMEM] + vmem_specs(8),
        out_specs=pl.BlockSpec(memory_space=pltpu.VMEM),
        scratch_shapes=[pltpu.VMEM((rows, 2 * hid), BF)],
        compiler_params=pltpu.CompilerParams(vmem_limit_bytes=24 * MIB),
        cost_estimate=pl.CostEstimate(
            flops=4 * rows * hid * width, bytes_accessed=6 * MIB, transcendentals=0
        ),
    )(at, *pieces, low, high)


def last_kernel(got_ref, stream_ref, o_ref):
    total = stream_ref[...]
    for i in range(NQ):
        total = total + got_ref[i].astype(F32)
    nm = o_ref.shape[0]
    r = o_ref.shape[1] // N_FFN
    for m in range(nm):
        rows = [total[(j * nm + m) * r : (j * nm + m + 1) * r] for j in range(N_FFN)]
        o_ref[m] = jnp.concatenate(rows, axis=0).astype(BF)


def last(got, stream, nm):
    rows, width = stream.shape
    return pl.pallas_call(
        last_kernel,
        out_shape=jax.ShapeDtypeStruct((nm, rows // nm, width), BF),
        in_specs=vmem_specs(2),
        out_specs=pl.BlockSpec(memory_space=pltpu.VMEM),
        compiler_params=pltpu.CompilerParams(vmem_limit_bytes=16 * MIB),
    )(got, stream)


def by_core(a, own, sib):
    return jnp.where(a % 2 == 0, own, sib), jnp.where(a % 2 == 0, sib, own)


def scatter_ffn(sends, keeps):
    f = lambda t: t.astype(F32)
    r1 = [fx(s, o[0]) for s, o in zip(sends, ORDER)]
    s2 = [(f(k[1]) + f(r[1])).astype(BF) for k, r in zip(keeps, r1)]
    r2 = [fx(s, o[1]) for s, o in zip(s2, ORDER)]
    s3 = [(f(k[0, 1]) + f(r[0, 1]) + f(q[1])).astype(BF) for k, r, q in zip(keeps, r1, r2)]
    r3 = [fx(s, o[2]) for s, o in zip(s3, ORDER)]
    return [
        f(k[0, 0]) + f(r[0, 0]) + f(q[0]) + f(t) for k, r, q, t in zip(keeps, r1, r2, r3)
    ]


def gather_ffn(parts):
    s = [jnp.stack([x, fx(x, o[2])]) for x, o in zip(parts, ORDER)]
    s = [jnp.stack([x, fx(x, o[1])]) for x, o in zip(s, ORDER)]
    return [t for x, o in zip(s, ORDER) for t in (x, fx(x, o[0]))]


def local(
    queries,
    cache_keys,
    cache_values,
    lengths,
    residual,
    norm_gain,
    out_weight,
    gate_weight,
    up_weight,
    down_weight,
):
    nm, r = queries.shape[:2]
    n = nm * r
    a = lax.axis_index("attn")
    f = lax.axis_index("ffn")
    at = jnp.stack([a % 2, f, a // 2]).astype(jnp.int32)
    w = residual.shape[2]
    rows = N_FFN * n

    out_sib = ax(out_weight, 1)
    gate_sib = ax(gate_weight, 1)
    up_sib = ax(up_weight, 1)
    down_sib = ax(down_weight, 1)

    res = lax.dynamic_slice_in_dim(residual, a * (N_FFN * r), N_FFN * r, 1)
    res = res.reshape(nm, N_FFN, r, w).transpose(1, 0, 2, 3).reshape(rows, w)
    gain = norm_gain.reshape(1, w)

    out = attend(queries, cache_keys, cache_values, lengths)
    got = over_chips(out.reshape(n, NQ, -1).transpose(1, 0, 2)).reshape(NQ * n, -1)

    got, out_sib, gate_sib, up_sib, down_sib = lax.optimization_barrier(
        (got, out_sib, gate_sib, up_sib, down_sib)
    )
    pieces = gather_ffn([got[:, x:y] for x, y in zip(PROJECT_CUTS, PROJECT_CUTS[1:])])
    part = project(at, pieces, *by_core(a, out_weight, out_sib))
    stream, scaled = residual_stream(over_chips(part), res, gain)

    pair = jnp.stack([scaled, ax(scaled, 8)])
    pieces = [pair] + [ax(pair, 2 * k) for k in range(1, 4)]
    gate0, gate1 = by_core(a, gate_weight, gate_sib)
    up0, up1 = by_core(a, up_weight, up_sib)
    sends, keeps = hidden(at, pieces, gain, (gate0, up0, gate1, up1))
    sums = scatter_ffn(sends, keeps)
    step = gate_weight.shape[1] // NP
    inv = lax.rsqrt(sums[SQUARE_PART][:, 4 * step : 4 * step + 1] / D + 1e-06)
    acts = []
    for t in sums:
        g0, u0, g1, u1 = [t[:, i * step : (i + 1) * step] * inv for i in range(4)]
        acts.append(
            jnp.concatenate([jax.nn.silu(g0) * u0, jax.nn.silu(g1) * u1], axis=1).astype(BF)
        )
    part = down(at, gather_ffn(acts), *by_core(a, down_weight, down_sib)).reshape(NQ, rows, w)
    return last(over_chips(part), stream, nm)


def solution(mesh):
    in_specs = (
        P(None, ("attn", "ffn"), None, None),
        P(None, ("attn", "ffn"), None, None),
        P(None, ("attn", "ffn"), None, None),
        P(None, ("attn", "ffn")),
        P(None, None, "ffn"),
        P("ffn"),
        P("attn", "ffn"),
        P("ffn", "attn"),
        P("ffn", "attn"),
        P("attn", "ffn"),
    )
    out_specs = P(None, "attn", "ffn")
    return jax.shard_map(local, mesh=mesh, in_specs=in_specs, out_specs=out_specs, check_vma=False)
```

```python
import functools
import math

import jax
import jax.numpy as jnp
from jax import lax
from jax.experimental import pallas as pl
from jax.experimental.pallas import tpu as pltpu
from jax.sharding import PartitionSpec as P

D = 7168
QB = 128
N_ATTN = 16
N_FFN = 8
NQ = 8
NEG = -1e30
BF = jnp.bfloat16
F32 = jnp.float32
MIB = 2**20
PLANES = [[2 * q + c for q in range(NQ)] for c in range(2)]
ORDER = ((1, 3, 4), (3, 4, 1), (4, 1, 3))
NP = len(ORDER)


def attend_kernel(len_ref, q_ref, k_hbm, v_hbm, o_ref, k_ref, v_ref, rows_ref, k_sem, v_sem):
    nm, r, h, hd = q_ref.shape
    l = k_ref.shape[1]
    for i in range(nm * r):
        m, t = divmod(i, r)
        pltpu.make_async_copy(k_hbm.at[m, t], k_ref.at[i], k_sem.at[i]).start()
        pltpu.make_async_copy(v_hbm.at[m, t], v_ref.at[i], v_sem.at[i]).start()
    offsets = lax.broadcasted_iota(jnp.int32, (h, l), 1)

    for step in range(nm * r // 2):
        outs = []
        for u in range(2):
            i = step * 2 + u
            m, t = i // r, i % r
            pltpu.make_async_copy(k_hbm.at[m, t], k_ref.at[i], k_sem.at[i]).wait()
            pltpu.make_async_copy(v_hbm.at[m, t], v_ref.at[i], v_sem.at[i]).wait()
        for u in range(2):
            i = step * 2 + u
            m, t = i // r, i % r
            scores = lax.dot_general(
                q_ref[m, t], k_ref[i], (((1,), (1,)), ((), ())), preferred_element_type=F32
            ) * (1.0 / math.sqrt(hd))
            scores = jnp.where(offsets < len_ref[m, t], scores, NEG)
            weights = jnp.exp(scores - jnp.max(scores, axis=1, keepdims=True))
            totals = jnp.sum(weights, axis=1, keepdims=True)
            outs.append(
                jnp.dot(weights.astype(BF), v_ref[i], preferred_element_type=F32) / totals
            )
        for u in range(2):
            for b in range(hd // QB):
                cols = slice(b * QB, (b + 1) * QB)
                block = outs[u][:, cols]
                peak = jnp.max(jnp.abs(block), axis=1, keepdims=True)
                scale = (peak + 1e-06).astype(BF).astype(F32)
                levels = jnp.clip(jnp.floor(127.0 * block / scale + 0.5), -127.0, 127.0)
                value = levels * scale / 127.0
                for head in range(h):
                    chip, at = divmod(head, h // NQ)
                    lanes = slice(at * hd + b * QB, at * hd + (b + 1) * QB)
                    rows_ref[chip, step * 2 + u : step * 2 + u + 1, lanes] = value[head : head + 1]

    o_ref[...] = rows_ref[...].astype(BF)


def attend(q, k, v, lengths):
    nm, r, h, hd = q.shape
    n, l = nm * r, k.shape[2]
    return pl.pallas_call(
        attend_kernel,
        out_shape=jax.ShapeDtypeStruct((NQ, n, h * hd // NQ), BF),
        in_specs=[
            pl.BlockSpec(memory_space=pltpu.SMEM),
            pl.BlockSpec(memory_space=pltpu.VMEM),
            pl.BlockSpec(memory_space=pltpu.HBM),
            pl.BlockSpec(memory_space=pltpu.HBM),
        ],
        out_specs=pl.BlockSpec(memory_space=pltpu.VMEM),
        scratch_shapes=[
            pltpu.VMEM((n, l, hd), BF),
            pltpu.VMEM((n, l, hd), BF),
            pltpu.VMEM((NQ, n, h * hd // NQ), F32),
            pltpu.SemaphoreType.DMA((n,)),
            pltpu.SemaphoreType.DMA((n,)),
        ],
        compiler_params=pltpu.CompilerParams(vmem_limit_bytes=58 * MIB),
        cost_estimate=pl.CostEstimate(
            flops=4 * n * h * l * hd, bytes_accessed=4 * n * l * hd, transcendentals=n * h * l
        ),
    )(lengths, q, k, v)


def ax(x, k):
    return lax.ppermute(x, "attn", [(i, i ^ k) for i in range(N_ATTN)])


def fx(x, k):
    return lax.ppermute(x, "ffn", [(i, i ^ k) for i in range(N_FFN)])


def over_chips(x):
    return lax.all_to_all(x, "attn", 0, 0, axis_index_groups=PLANES)


def vmem_specs(count):
    return [pl.BlockSpec(memory_space=pltpu.VMEM)] * count


SMEM = pl.BlockSpec(memory_space=pltpu.SMEM)


def column_chunks(width, step=256):
    return [(s, min(step, width - s)) for s in range(0, width, step)]


def rows_at(start, size):
    return pl.ds(pl.multiple_of(start, size), size)


def spread(at_ref, x_ref, groups, put):
    f = at_ref[1]
    per = x_ref.shape[0] // N_FFN
    for p, (near, far) in enumerate(zip(groups[0::2], groups[1::2])):
        o = ORDER[p]
        for b0, ref in enumerate((near, far)):
            for b1 in range(2):
                for b2 in range(2):
                    j = (b0 * o[0]) ^ (b1 * o[1]) ^ (b2 * o[2])
                    put(rows_at((f ^ j) * per, per), p, ref[b1, b2])


def project_kernel(at_ref, s0, r0, s1, r1, s2, r2, low_ref, high_ref, o_ref, x_ref):
    def put(rows, p, piece):
        x_ref[rows, PROJECT_CUTS[p] : PROJECT_CUTS[p + 1]] = piece

    spread(at_ref, x_ref, (s0, r0, s1, r1, s2, r2), put)
    depth = low_ref.shape[0]
    low, high = x_ref[:, :depth], x_ref[:, depth:]
    for start, size in column_chunks(o_ref.shape[2]):
        cols = slice(start, start + size)
        acc = jnp.dot(low, low_ref[:, cols], preferred_element_type=F32) + jnp.dot(
            high, high_ref[:, cols], preferred_element_type=F32
        )
        for q in range(NQ):
            for t in range(4):
                first = 2 * t * 64 + q * 8
                o_ref[q, t * 16 : t * 16 + 16, cols] = jnp.concatenate(
                    [acc[first : first + 8], acc[first + 64 : first + 72]], axis=0
                ).astype(BF)


def project(at, pieces, low, high):
    depth, width = low.shape
    rows = NQ * 64
    return pl.pallas_call(
        project_kernel,
        out_shape=jax.ShapeDtypeStruct((NQ, 64, width), BF),
        in_specs=[SMEM] + vmem_specs(8),
        out_specs=pl.BlockSpec(memory_space=pltpu.VMEM),
        scratch_shapes=[pltpu.VMEM((rows, 2 * depth), BF)],
        compiler_params=pltpu.CompilerParams(vmem_limit_bytes=24 * MIB),
        cost_estimate=pl.CostEstimate(
            flops=4 * rows * depth * width, bytes_accessed=6 * MIB, transcendentals=0
        ),
    )(at, *pieces, low, high)


def stream_kernel(got_ref, res_ref, gain_ref, stream_ref, scaled_ref):
    total = res_ref[...].astype(F32)
    for i in range(NQ):
        total = total + got_ref[i].astype(F32)
    stream_ref[...] = total
    scaled_ref[...] = (total * gain_ref[...].astype(F32)).astype(BF)


def residual_stream(got, res, gain):
    _, rows, width = got.shape
    return pl.pallas_call(
        stream_kernel,
        out_shape=(
            jax.ShapeDtypeStruct((rows, width), F32),
            jax.ShapeDtypeStruct((rows, width), BF),
        ),
        in_specs=vmem_specs(3),
        out_specs=tuple(vmem_specs(2)),
        compiler_params=pltpu.CompilerParams(vmem_limit_bytes=16 * MIB),
    )(got, res, gain)


def hidden_kernel(at_ref, p0, p1, p2, p3, gain_ref, g0, u0, g1, u1, *refs):
    outs, x_ref = refs[:-1], refs[-1]
    step = g0.shape[1] // NP
    f, q = at_ref[1], at_ref[2]
    for k, ref in enumerate((p0, p1, p2, p3)):
        for z in range(2):
            x_ref[rows_at((f ^ q ^ (z * 4 + k)) * 64, 64), :] = ref[z]
    full = x_ref[...]

    def put(acc, part, start):
        o = ORDER[part]
        cols = slice(start, start + acc.shape[1])
        for b0 in range(2):
            ref = outs[2 * part + 1 - b0]
            for b1 in range(2):
                for b2 in range(2):
                    j = (b0 * o[0]) ^ (b1 * o[1]) ^ (b2 * o[2])
                    ref[b1, b2, :, cols] = acc[j * 64 : j * 64 + 64].astype(BF)

    ratio = full.astype(F32) / gain_ref[...].astype(F32)
    square = jnp.sum(ratio * ratio, axis=1, keepdims=True)
    put(jnp.broadcast_to(square, (full.shape[0], 128)), SQUARE_PART, 4 * step)
    for i, w in enumerate((g0, u0, g1, u1)):
        acc = jnp.dot(full, w[...], preferred_element_type=F32)
        for part in range(NP):
            put(acc[:, part * step : (part + 1) * step], part, i * step)


SQUARE_PART = 2
PROJECT_CUTS = (0, 768, 1408, 2048)


def hidden(at, pieces, gain, weights):
    width, hid = weights[0].shape
    step, rows = hid // NP, NQ * 64
    shapes = []
    for part in range(NP):
        cols = 4 * step + (128 if part == SQUARE_PART else 0)
        shapes += [jax.ShapeDtypeStruct((2, 2, 64, cols), BF)] * 2
    outs = pl.pallas_call(
        hidden_kernel,
        out_shape=tuple(shapes),
        in_specs=[SMEM] + vmem_specs(9),
        out_specs=tuple(vmem_specs(2 * NP)),
        scratch_shapes=[pltpu.VMEM((rows, width), BF)],
        compiler_params=pltpu.CompilerParams(vmem_limit_bytes=24 * MIB),
        cost_estimate=pl.CostEstimate(
            flops=8 * rows * width * hid, bytes_accessed=14 * MIB, transcendentals=0
        ),
    )(at, *pieces, gain, *weights)
    return outs[0::2], outs[1::2]


def down_kernel(at_ref, s0, r0, s1, r1, s2, r2, low_ref, high_ref, o_ref, x_ref):
    hid = low_ref.shape[0]
    step = hid // NP

    def put(rows, p, piece):
        x_ref[rows, p * step : (p + 1) * step] = piece[:, :step]
        x_ref[rows, hid + p * step : hid + (p + 1) * step] = piece[:, step:]

    spread(at_ref, x_ref, (s0, r0, s1, r1, s2, r2), put)
    low, high = x_ref[:, :hid], x_ref[:, hid:]
    for start, size in column_chunks(o_ref.shape[1]):
        cols = slice(start, start + size)
        acc = jnp.dot(low, low_ref[:, cols], preferred_element_type=F32) + jnp.dot(
            high, high_ref[:, cols], preferred_element_type=F32
        )
        o_ref[:, cols] = acc.astype(BF)


def down(at, pieces, low, high):
    hid, width = low.shape
    rows = NQ * pieces[0].shape[2]
    return pl.pallas_call(
        down_kernel,
        out_shape=jax.ShapeDtypeStruct((rows, width), BF),
        in_specs=[SMEM] + vmem_specs(8),
        out_specs=pl.BlockSpec(memory_space=pltpu.VMEM),
        scratch_shapes=[pltpu.VMEM((rows, 2 * hid), BF)],
        compiler_params=pltpu.CompilerParams(vmem_limit_bytes=24 * MIB),
        cost_estimate=pl.CostEstimate(
            flops=4 * rows * hid * width, bytes_accessed=6 * MIB, transcendentals=0
        ),
    )(at, *pieces, low, high)


def last_kernel(got_ref, stream_ref, o_ref):
    total = stream_ref[...]
    for i in range(NQ):
        total = total + got_ref[i].astype(F32)
    nm = o_ref.shape[0]
    r = o_ref.shape[1] // N_FFN
    for m in range(nm):
        rows = [total[(j * nm + m) * r : (j * nm + m + 1) * r] for j in range(N_FFN)]
        o_ref[m] = jnp.concatenate(rows, axis=0).astype(BF)


def last(got, stream, nm):
    rows, width = stream.shape
    return pl.pallas_call(
        last_kernel,
        out_shape=jax.ShapeDtypeStruct((nm, rows // nm, width), BF),
        in_specs=vmem_specs(2),
        out_specs=pl.BlockSpec(memory_space=pltpu.VMEM),
        compiler_params=pltpu.CompilerParams(vmem_limit_bytes=16 * MIB),
    )(got, stream)


def by_core(a, own, sib):
    return jnp.where(a % 2 == 0, own, sib), jnp.where(a % 2 == 0, sib, own)


def scatter_ffn(sends, keeps):
    f = lambda t: t.astype(F32)
    r1 = [fx(s, o[0]) for s, o in zip(sends, ORDER)]
    s2 = [(f(k[1]) + f(r[1])).astype(BF) for k, r in zip(keeps, r1)]
    r2 = [fx(s, o[1]) for s, o in zip(s2, ORDER)]
    s3 = [(f(k[0, 1]) + f(r[0, 1]) + f(q[1])).astype(BF) for k, r, q in zip(keeps, r1, r2)]
    r3 = [fx(s, o[2]) for s, o in zip(s3, ORDER)]
    return [
        f(k[0, 0]) + f(r[0, 0]) + f(q[0]) + f(t) for k, r, q, t in zip(keeps, r1, r2, r3)
    ]


def gather_ffn(parts):
    s = [jnp.stack([x, fx(x, o[2])]) for x, o in zip(parts, ORDER)]
    s = [jnp.stack([x, fx(x, o[1])]) for x, o in zip(s, ORDER)]
    return [t for x, o in zip(s, ORDER) for t in (x, fx(x, o[0]))]


def local(
    queries,
    cache_keys,
    cache_values,
    lengths,
    residual,
    norm_gain,
    out_weight,
    gate_weight,
    up_weight,
    down_weight,
):
    nm, r = queries.shape[:2]
    n = nm * r
    a = lax.axis_index("attn")
    f = lax.axis_index("ffn")
    at = jnp.stack([a % 2, f, a // 2]).astype(jnp.int32)
    w = residual.shape[2]
    rows = N_FFN * n

    out_sib = ax(out_weight, 1)
    gate_sib = ax(gate_weight, 1)
    up_sib = ax(up_weight, 1)
    down_sib = ax(down_weight, 1)

    res = lax.dynamic_slice_in_dim(residual, a * (N_FFN * r), N_FFN * r, 1)
    res = res.reshape(nm, N_FFN, r, w).transpose(1, 0, 2, 3).reshape(rows, w)
    gain = norm_gain.reshape(1, w)

    out = attend(queries, cache_keys, cache_values, lengths)
    got = over_chips(out).reshape(NQ * n, -1)

    got, out_sib, gate_sib, up_sib, down_sib = lax.optimization_barrier(
        (got, out_sib, gate_sib, up_sib, down_sib)
    )
    pieces = gather_ffn([got[:, x:y] for x, y in zip(PROJECT_CUTS, PROJECT_CUTS[1:])])
    part = project(at, pieces, *by_core(a, out_weight, out_sib))
    stream, scaled = residual_stream(over_chips(part), res, gain)

    pair = jnp.stack([scaled, ax(scaled, 8)])
    pieces = [pair] + [ax(pair, 2 * k) for k in range(1, 4)]
    gate0, gate1 = by_core(a, gate_weight, gate_sib)
    up0, up1 = by_core(a, up_weight, up_sib)
    sends, keeps = hidden(at, pieces, gain, (gate0, up0, gate1, up1))
    sums = scatter_ffn(sends, keeps)
    step = gate_weight.shape[1] // NP
    inv = lax.rsqrt(sums[SQUARE_PART][:, 4 * step : 4 * step + 1] / D + 1e-06)
    acts = []
    for t in sums:
        g0, u0, g1, u1 = [t[:, i * step : (i + 1) * step] * inv for i in range(4)]
        acts.append(
            jnp.concatenate([jax.nn.silu(g0) * u0, jax.nn.silu(g1) * u1], axis=1).astype(BF)
        )
    part = down(at, gather_ffn(acts), *by_core(a, down_weight, down_sib)).reshape(NQ, rows, w)
    return last(over_chips(part), stream, nm)


def solution(mesh):
    in_specs = (
        P(None, ("attn", "ffn"), None, None),
        P(None, ("attn", "ffn"), None, None),
        P(None, ("attn", "ffn"), None, None),
        P(None, ("attn", "ffn")),
        P(None, None, "ffn"),
        P("ffn"),
        P("attn", "ffn"),
        P("ffn", "attn"),
        P("ffn", "attn"),
        P("attn", "ffn"),
    )
    out_specs = P(None, "attn", "ffn")
    return jax.shard_map(local, mesh=mesh, in_specs=in_specs, out_specs=out_specs, check_vma=False)
```

```python
import functools
import math

import jax
import jax.numpy as jnp
from jax import lax
from jax.experimental import pallas as pl
from jax.experimental.pallas import tpu as pltpu
from jax.sharding import PartitionSpec as P

D = 7168
QB = 128
N_ATTN = 16
N_FFN = 8
NQ = 8
NEG = -1e30
BF = jnp.bfloat16
F32 = jnp.float32
MIB = 2**20
PLANES = [[2 * q + c for q in range(NQ)] for c in range(2)]
ORDER = ((4, 1, 3), (1, 3, 4), (3, 4, 1))
NP = len(ORDER)


ATTEND_GROUPS = ((0,), (1,), (2, 3), (4, 5, 6, 7))


def attend_kernel(len_ref, q_ref, k_hbm, v_hbm, o_ref, k_ref, v_ref, rows_ref, k_sem, v_sem):
    nm, r, h, hd = q_ref.shape
    l = k_ref.shape[1]
    for i in range(nm * r):
        m, t = divmod(i, r)
        pltpu.make_async_copy(k_hbm.at[m, t], k_ref.at[i], k_sem.at[i]).start()
        pltpu.make_async_copy(v_hbm.at[m, t], v_ref.at[i], v_sem.at[i]).start()
    offsets = lax.broadcasted_iota(jnp.int32, (h, l), 1)

    for group in ATTEND_GROUPS:
        outs = []
        for i in group:
            m, t = i // r, i % r
            pltpu.make_async_copy(k_hbm.at[m, t], k_ref.at[i], k_sem.at[i]).wait()
            pltpu.make_async_copy(v_hbm.at[m, t], v_ref.at[i], v_sem.at[i]).wait()
        for i in group:
            m, t = i // r, i % r
            scores = lax.dot_general(
                q_ref[m, t], k_ref[i], (((1,), (1,)), ((), ())), preferred_element_type=F32
            ) * (1.0 / math.sqrt(hd))
            scores = jnp.where(offsets < len_ref[m, t], scores, NEG)
            weights = jnp.exp(scores - jnp.max(scores, axis=1, keepdims=True))
            totals = jnp.sum(weights, axis=1, keepdims=True)
            outs.append(
                jnp.dot(weights.astype(BF), v_ref[i], preferred_element_type=F32) / totals
            )
        for i, out in zip(group, outs):
            for b in range(hd // QB):
                cols = slice(b * QB, (b + 1) * QB)
                block = out[:, cols]
                peak = jnp.max(jnp.abs(block), axis=1, keepdims=True)
                scale = (peak + 1e-06).astype(BF).astype(F32)
                levels = jnp.clip(jnp.floor(127.0 * block / scale + 0.5), -127.0, 127.0)
                value = levels * scale / 127.0
                for head in range(h):
                    chip, at = divmod(head, h // NQ)
                    lanes = slice(at * hd + b * QB, at * hd + (b + 1) * QB)
                    rows_ref[chip, i : i + 1, lanes] = value[head : head + 1]

    o_ref[...] = rows_ref[...].astype(BF)


def attend(q, k, v, lengths):
    nm, r, h, hd = q.shape
    n, l = nm * r, k.shape[2]
    return pl.pallas_call(
        attend_kernel,
        out_shape=jax.ShapeDtypeStruct((NQ, n, h * hd // NQ), BF),
        in_specs=[
            pl.BlockSpec(memory_space=pltpu.SMEM),
            pl.BlockSpec(memory_space=pltpu.VMEM),
            pl.BlockSpec(memory_space=pltpu.HBM),
            pl.BlockSpec(memory_space=pltpu.HBM),
        ],
        out_specs=pl.BlockSpec(memory_space=pltpu.VMEM),
        scratch_shapes=[
            pltpu.VMEM((n, l, hd), BF),
            pltpu.VMEM((n, l, hd), BF),
            pltpu.VMEM((NQ, n, h * hd // NQ), F32),
            pltpu.SemaphoreType.DMA((n,)),
            pltpu.SemaphoreType.DMA((n,)),
        ],
        compiler_params=pltpu.CompilerParams(vmem_limit_bytes=58 * MIB),
        cost_estimate=pl.CostEstimate(
            flops=4 * n * h * l * hd, bytes_accessed=4 * n * l * hd, transcendentals=n * h * l
        ),
    )(lengths, q, k, v)


def ax(x, k):
    return lax.ppermute(x, "attn", [(i, i ^ k) for i in range(N_ATTN)])


def fx(x, k):
    return lax.ppermute(x, "ffn", [(i, i ^ k) for i in range(N_FFN)])


def over_chips(x):
    return lax.all_to_all(x, "attn", 0, 0, axis_index_groups=PLANES)


def vmem_specs(count):
    return [pl.BlockSpec(memory_space=pltpu.VMEM)] * count


SMEM = pl.BlockSpec(memory_space=pltpu.SMEM)


def column_chunks(width, step=256):
    return [(s, min(step, width - s)) for s in range(0, width, step)]


def rows_at(start, size):
    return pl.ds(pl.multiple_of(start, size), size)


def spread(at_ref, x_ref, groups, put):
    f = at_ref[1]
    per = x_ref.shape[0] // N_FFN
    for p, (near, far) in enumerate(zip(groups[0::2], groups[1::2])):
        o = ORDER[p]
        for b0, ref in enumerate((near, far)):
            for b1 in range(2):
                for b2 in range(2):
                    j = (b0 * o[0]) ^ (b1 * o[1]) ^ (b2 * o[2])
                    put(rows_at((f ^ j) * per, per), p, ref[b1, b2])


def project_kernel(at_ref, s0, r0, s1, r1, s2, r2, low_ref, high_ref, o_ref, x_ref):
    def put(rows, p, piece):
        x_ref[rows, PROJECT_CUTS[p] : PROJECT_CUTS[p + 1]] = piece

    spread(at_ref, x_ref, (s0, r0, s1, r1, s2, r2), put)
    depth = low_ref.shape[0]
    low, high = x_ref[:, :depth], x_ref[:, depth:]
    for start, size in column_chunks(o_ref.shape[2]):
        cols = slice(start, start + size)
        acc = jnp.dot(low, low_ref[:, cols], preferred_element_type=F32) + jnp.dot(
            high, high_ref[:, cols], preferred_element_type=F32
        )
        for q in range(NQ):
            for t in range(4):
                first = 2 * t * 64 + q * 8
                o_ref[q, t * 16 : t * 16 + 16, cols] = jnp.concatenate(
                    [acc[first : first + 8], acc[first + 64 : first + 72]], axis=0
                ).astype(BF)


def project(at, pieces, low, high):
    depth, width = low.shape
    rows = NQ * 64
    return pl.pallas_call(
        project_kernel,
        out_shape=jax.ShapeDtypeStruct((NQ, 64, width), BF),
        in_specs=[SMEM] + vmem_specs(8),
        out_specs=pl.BlockSpec(memory_space=pltpu.VMEM),
        scratch_shapes=[pltpu.VMEM((rows, 2 * depth), BF)],
        compiler_params=pltpu.CompilerParams(vmem_limit_bytes=24 * MIB),
        cost_estimate=pl.CostEstimate(
            flops=4 * rows * depth * width, bytes_accessed=6 * MIB, transcendentals=0
        ),
    )(at, *pieces, low, high)


def stream_kernel(got_ref, res_ref, gain_ref, stream_ref, scaled_ref):
    total = res_ref[...].astype(F32)
    for i in range(NQ):
        total = total + got_ref[i].astype(F32)
    stream_ref[...] = total
    scaled_ref[...] = (total * gain_ref[...].astype(F32)).astype(BF)


def residual_stream(got, res, gain):
    _, rows, width = got.shape
    return pl.pallas_call(
        stream_kernel,
        out_shape=(
            jax.ShapeDtypeStruct((rows, width), F32),
            jax.ShapeDtypeStruct((rows, width), BF),
        ),
        in_specs=vmem_specs(3),
        out_specs=tuple(vmem_specs(2)),
        compiler_params=pltpu.CompilerParams(vmem_limit_bytes=16 * MIB),
    )(got, res, gain)


def hidden_kernel(at_ref, p0, p1, p2, p3, gain_ref, g0, u0, g1, u1, *refs):
    outs, x_ref = refs[:-1], refs[-1]
    step = g0.shape[1] // NP
    f, q = at_ref[1], at_ref[2]
    for k, ref in enumerate((p0, p1, p2, p3)):
        for z in range(2):
            x_ref[rows_at((f ^ q ^ (z * 4 + k)) * 64, 64), :] = ref[z]
    full = x_ref[...]

    def put(acc, part, start):
        o = ORDER[part]
        cols = slice(start, start + acc.shape[1])
        for b0 in range(2):
            ref = outs[2 * part + 1 - b0]
            for b1 in range(2):
                for b2 in range(2):
                    j = (b0 * o[0]) ^ (b1 * o[1]) ^ (b2 * o[2])
                    ref[b1, b2, :, cols] = acc[j * 64 : j * 64 + 64].astype(BF)

    ratio = full.astype(F32) / gain_ref[...].astype(F32)
    square = jnp.sum(ratio * ratio, axis=1, keepdims=True)
    put(jnp.broadcast_to(square, (full.shape[0], 128)), SQUARE_PART, 4 * step)
    for i, w in enumerate((g0, u0, g1, u1)):
        acc = jnp.dot(full, w[...], preferred_element_type=F32)
        for part in range(NP):
            put(acc[:, part * step : (part + 1) * step], part, i * step)


SQUARE_PART = 2
PROJECT_CUTS = (0, 768, 1408, 2048)


def hidden(at, pieces, gain, weights):
    width, hid = weights[0].shape
    step, rows = hid // NP, NQ * 64
    shapes = []
    for part in range(NP):
        cols = 4 * step + (128 if part == SQUARE_PART else 0)
        shapes += [jax.ShapeDtypeStruct((2, 2, 64, cols), BF)] * 2
    outs = pl.pallas_call(
        hidden_kernel,
        out_shape=tuple(shapes),
        in_specs=[SMEM] + vmem_specs(9),
        out_specs=tuple(vmem_specs(2 * NP)),
        scratch_shapes=[pltpu.VMEM((rows, width), BF)],
        compiler_params=pltpu.CompilerParams(vmem_limit_bytes=24 * MIB),
        cost_estimate=pl.CostEstimate(
            flops=8 * rows * width * hid, bytes_accessed=14 * MIB, transcendentals=0
        ),
    )(at, *pieces, gain, *weights)
    return outs[0::2], outs[1::2]


def down_kernel(at_ref, s0, r0, s1, r1, s2, r2, low_ref, high_ref, o_ref, x_ref):
    hid = low_ref.shape[0]
    step = hid // NP

    def put(rows, p, piece):
        x_ref[rows, p * step : (p + 1) * step] = piece[:, :step]
        x_ref[rows, hid + p * step : hid + (p + 1) * step] = piece[:, step:]

    spread(at_ref, x_ref, (s0, r0, s1, r1, s2, r2), put)
    low, high = x_ref[:, :hid], x_ref[:, hid:]
    for start, size in column_chunks(o_ref.shape[1]):
        cols = slice(start, start + size)
        acc = jnp.dot(low, low_ref[:, cols], preferred_element_type=F32) + jnp.dot(
            high, high_ref[:, cols], preferred_element_type=F32
        )
        o_ref[:, cols] = acc.astype(BF)


def down(at, pieces, low, high):
    hid, width = low.shape
    rows = NQ * pieces[0].shape[2]
    return pl.pallas_call(
        down_kernel,
        out_shape=jax.ShapeDtypeStruct((rows, width), BF),
        in_specs=[SMEM] + vmem_specs(8),
        out_specs=pl.BlockSpec(memory_space=pltpu.VMEM),
        scratch_shapes=[pltpu.VMEM((rows, 2 * hid), BF)],
        compiler_params=pltpu.CompilerParams(vmem_limit_bytes=24 * MIB),
        cost_estimate=pl.CostEstimate(
            flops=4 * rows * hid * width, bytes_accessed=6 * MIB, transcendentals=0
        ),
    )(at, *pieces, low, high)


def last_kernel(got_ref, stream_ref, o_ref):
    total = stream_ref[...]
    for i in range(NQ):
        total = total + got_ref[i].astype(F32)
    nm = o_ref.shape[0]
    r = o_ref.shape[1] // N_FFN
    for m in range(nm):
        rows = [total[(j * nm + m) * r : (j * nm + m + 1) * r] for j in range(N_FFN)]
        o_ref[m] = jnp.concatenate(rows, axis=0).astype(BF)


def last(got, stream, nm):
    rows, width = stream.shape
    return pl.pallas_call(
        last_kernel,
        out_shape=jax.ShapeDtypeStruct((nm, rows // nm, width), BF),
        in_specs=vmem_specs(2),
        out_specs=pl.BlockSpec(memory_space=pltpu.VMEM),
        compiler_params=pltpu.CompilerParams(vmem_limit_bytes=16 * MIB),
    )(got, stream)


def by_core(a, own, sib):
    return jnp.where(a % 2 == 0, own, sib), jnp.where(a % 2 == 0, sib, own)


def scatter_ffn(sends, keeps):
    f = lambda t: t.astype(F32)
    r1 = [fx(s, o[0]) for s, o in zip(sends, ORDER)]
    s2 = [(f(k[1]) + f(r[1])).astype(BF) for k, r in zip(keeps, r1)]
    r2 = [fx(s, o[1]) for s, o in zip(s2, ORDER)]
    s3 = [(f(k[0, 1]) + f(r[0, 1]) + f(q[1])).astype(BF) for k, r, q in zip(keeps, r1, r2)]
    r3 = [fx(s, o[2]) for s, o in zip(s3, ORDER)]
    return [
        f(k[0, 0]) + f(r[0, 0]) + f(q[0]) + f(t) for k, r, q, t in zip(keeps, r1, r2, r3)
    ]


def gather_ffn(parts):
    s = [jnp.stack([x, fx(x, o[2])]) for x, o in zip(parts, ORDER)]
    s = [jnp.stack([x, fx(x, o[1])]) for x, o in zip(s, ORDER)]
    return [t for x, o in zip(s, ORDER) for t in (x, fx(x, o[0]))]


def local(
    queries,
    cache_keys,
    cache_values,
    lengths,
    residual,
    norm_gain,
    out_weight,
    gate_weight,
    up_weight,
    down_weight,
):
    nm, r = queries.shape[:2]
    n = nm * r
    a = lax.axis_index("attn")
    f = lax.axis_index("ffn")
    at = jnp.stack([a % 2, f, a // 2]).astype(jnp.int32)
    w = residual.shape[2]
    rows = N_FFN * n

    out_sib = ax(out_weight, 1)
    gate_sib = ax(gate_weight, 1)
    up_sib = ax(up_weight, 1)
    down_sib = ax(down_weight, 1)

    res = lax.dynamic_slice_in_dim(residual, a * (N_FFN * r), N_FFN * r, 1)
    res = res.reshape(nm, N_FFN, r, w).transpose(1, 0, 2, 3).reshape(rows, w)
    gain = norm_gain.reshape(1, w)

    out = attend(queries, cache_keys, cache_values, lengths)
    got = over_chips(out).reshape(NQ * n, -1)

    got, out_sib, gate_sib, up_sib, down_sib, res, gain, at = lax.optimization_barrier(
        (got, out_sib, gate_sib, up_sib, down_sib, res, gain, at)
    )
    pieces = gather_ffn([got[:, x:y] for x, y in zip(PROJECT_CUTS, PROJECT_CUTS[1:])])
    part = project(at, pieces, *by_core(a, out_weight, out_sib))
    stream, scaled = residual_stream(over_chips(part), res, gain)

    pair = jnp.stack([scaled, ax(scaled, 8)])
    pieces = [pair] + [ax(pair, 2 * k) for k in range(1, 4)]
    gate0, gate1 = by_core(a, gate_weight, gate_sib)
    up0, up1 = by_core(a, up_weight, up_sib)
    sends, keeps = hidden(at, pieces, gain, (gate0, up0, gate1, up1))
    sums = scatter_ffn(sends, keeps)
    step = gate_weight.shape[1] // NP
    inv = lax.rsqrt(sums[SQUARE_PART][:, 4 * step : 4 * step + 1] / D + 1e-06)
    acts = []
    for t in sums:
        g0, u0, g1, u1 = [t[:, i * step : (i + 1) * step] * inv for i in range(4)]
        acts.append(
            jnp.concatenate([jax.nn.silu(g0) * u0, jax.nn.silu(g1) * u1], axis=1).astype(BF)
        )
    part = down(at, gather_ffn(acts), *by_core(a, down_weight, down_sib)).reshape(NQ, rows, w)
    return last(over_chips(part), stream, nm)


def solution(mesh):
    in_specs = (
        P(None, ("attn", "ffn"), None, None),
        P(None, ("attn", "ffn"), None, None),
        P(None, ("attn", "ffn"), None, None),
        P(None, ("attn", "ffn")),
        P(None, None, "ffn"),
        P("ffn"),
        P("attn", "ffn"),
        P("ffn", "attn"),
        P("ffn", "attn"),
        P("attn", "ffn"),
    )
    out_specs = P(None, "attn", "ffn")
    return jax.shard_map(local, mesh=mesh, in_specs=in_specs, out_specs=out_specs, check_vma=False)
```
